32 devices in a mesh: grp: 2 (over y), tm: 4 (over z), feat: 2 (over x), rep: 2 (over core).
Axes of the slice: x: 2, y: 2, z: 4, core: 2. Of those that a mesh axis runs over, the one named last changes fastest.
Arguments:
- archive: float32 [128, 4, 3, 4096], P(('grp', 'tm'), ('feat', 'rep')), parts along dimension 0
- swap_history: int32 [128, 4], P(('grp', 'tm')), parts along dimension 0, may hold values from 0 to 3, as said below
- pair_index: int32 [2, 4096], replicated, may hold values from 0 to 4095
Outputs:
- inst_cov: float32 [8192, 4096], P(('grp', 'tm'), ('feat', 'rep')), parts along dimension 0
- lag_cov: float32 [8192, 4096], P(('grp', 'tm'), ('feat', 'rep')), parts along dimension 0
The draws below stay inside these ranges and needn't reach their ends.
There are 2 independent parts, one for each index of `grp`. The reference program is written for one: setup_inputs(seed, part) draws one part's arguments, and reference() takes and returns one part's arrays. A program takes and returns all parts, laid end to end along the dimension named above; an argument that names none is the same for every part. Nothing has to cross between parts.
Inputs may be any that keep to these rules, and one draw needn't show every extreme that they name: Each row swap_history[t, :] is a permutation of 0 to 3.
All inputs are finite; a program needn't handle non-finite values.
Results may differ from the reference program's by a relative error of at most 0.0027.
Values may be sent and summed in bfloat16 or wider, within the bound.
A program may use at most 128 MiB of HBM per device.

```python
import math
import jax
import jax.numpy as jnp
from jax import lax

RES = 4096
FEATS = 4096
LAG = 16
REPLICAS = 4
STEPS = 64


def history(key):
    step_keys = jax.random.split(jax.random.fold_in(key, 7), STEPS)

    def one_row(step_key):
        return jax.random.permutation(step_key, REPLICAS)
    return jax.vmap(one_row)(step_keys).astype(jnp.int32)


def draw_swap_history(key, part):
    return history(key)


def draw_archive(key, part):
    replica_order = history(key)
    shape_key = jax.random.fold_in(key, 13)
    noise_key = jax.random.fold_in(key, 17)
    wave_key = jax.random.fold_in(key, 19)
    shapes = jax.random.uniform(shape_key, (REPLICAS, 3, RES), jnp.float32, 0.0, 1.2)
    jitter = 0.1 * jax.random.normal(noise_key, (STEPS, REPLICAS, 3, RES), jnp.float32)
    amplitude = 0.2
    times = jnp.arange(STEPS, dtype=jnp.float32)
    trajectory = jnp.broadcast_to(shapes[None], (STEPS, REPLICAS, 3, RES)).astype(jnp.float32)
    for wave in range(3):
        period_key = jax.random.fold_in(wave_key, 3 * wave)
        sine_key = jax.random.fold_in(wave_key, 3 * wave + 1)
        cosine_key = jax.random.fold_in(wave_key, 3 * wave + 2)
        log_period = jax.random.uniform(period_key, (REPLICAS,), jnp.float32, math.log(20.0), math.log(200.0))
        period = jnp.exp(log_period)
        phase = 2.0 * math.pi * times[:, None] / period[None, :]
        coef_sine = amplitude * jax.random.normal(sine_key, (REPLICAS, 3, RES), jnp.float32)
        coef_cosine = amplitude * jax.random.normal(cosine_key, (REPLICAS, 3, RES), jnp.float32)
        trajectory = trajectory + jnp.sin(phase)[:, :, None, None] * coef_sine[None]
        trajectory = trajectory + jnp.cos(phase)[:, :, None, None] * coef_cosine[None]
    expanded = jnp.broadcast_to(replica_order[:, :, None, None], (STEPS, REPLICAS, 3, RES))
    by_state = jnp.take_along_axis(trajectory, expanded, axis=1)
    return (by_state + jitter).astype(jnp.float32)


def place_ends(values, own_key, least, top_value):
    longest = values.shape.index(max(values.shape))
    spots = []
    for shift in (0, 1):
        where = [jax.random.randint(jax.random.fold_in(own_key, axis), (), 0, length) for axis, length in enumerate(values.shape)]
        where[longest] = (where[longest] + shift) % values.shape[longest]
        spots.append(tuple(where))
    return values.at[spots[0]].set(least).at[spots[1]].set(top_value)


def setup_inputs(seed: int = 0, part: int = 0) -> dict:
    arg_keys = jax.random.split(jax.random.key(seed), 4)
    part_splits = jax.random.split(jax.random.fold_in(arg_keys[3], part), 4)
    return {
        "archive": draw_archive(jax.random.fold_in(jax.random.fold_in(arg_keys[3], part), 71), part),
        "swap_history": draw_swap_history(jax.random.fold_in(jax.random.fold_in(arg_keys[3], part), 71), part),
        "pair_index": place_ends(jax.random.randint(arg_keys[2], (2, FEATS), 0, RES), jax.random.fold_in(arg_keys[2], 1), 0, RES - 1).astype(jnp.int32),
    }


DIST_FLOOR = 0.3

def featurize(coords, pair_index):
    coords_one = jnp.take(coords, pair_index[0], axis=-1)
    coords_two = jnp.take(coords, pair_index[1], axis=-1)
    displace = coords_one - coords_two
    distance = jnp.sqrt(lax.optimization_barrier(jnp.sum(displace * displace, axis=-2)))
    return (1.0 / jnp.maximum(distance, DIST_FLOOR)).astype(jnp.bfloat16)

def holder_states(swap_rows, replicas):
    wanted = jnp.arange(replicas, dtype=jnp.int32)
    matches = swap_rows[:, :, None] == wanted[None, None, :]
    states = jnp.arange(replicas, dtype=jnp.int32)[None, :, None]
    return lax.optimization_barrier(jnp.sum(jnp.where(matches, states, 0), axis=1)).astype(jnp.int32)

def reference(archive, swap_history, pair_index):
    inverse = holder_states(swap_history, REPLICAS)

    def one_step(operands):
        step_frames, step_inverse = operands
        expanded = jnp.broadcast_to(step_inverse[:, None, None], step_frames.shape)
        ordered = jnp.take_along_axis(step_frames, expanded, axis=0)
        return featurize(ordered, pair_index)
    features = lax.map(one_step, (archive, inverse))
    kept_steps = STEPS - LAG
    frame_count = kept_steps * REPLICAS
    lead = features[:kept_steps].reshape(frame_count, FEATS)
    lagged = features[LAG:].reshape(frame_count, FEATS)
    mean_lead = lax.optimization_barrier(jnp.sum(lead, axis=0, dtype=jnp.float32)) / frame_count
    mean_lagged = lax.optimization_barrier(jnp.sum(lagged, axis=0, dtype=jnp.float32)) / frame_count
    inst_sum = jnp.dot(lead.T, lead, preferred_element_type=jnp.float32)
    lag_sum = jnp.dot(lead.T, lagged, preferred_element_type=jnp.float32)
    inst_cov = inst_sum / frame_count - mean_lead[:, None] * mean_lead[None, :]
    lag_cov = lag_sum / frame_count - mean_lead[:, None] * mean_lagged[None, :]
    return (inst_cov, lag_cov)
```

```python
import functools

import jax
import jax.numpy as jnp
from jax import lax
from jax.experimental import pallas as pl
from jax.experimental.pallas import tpu as pltpu
from jax.sharding import PartitionSpec as P

LAG = 16
DIST_FLOOR = 0.3
LANES = 128
SUBLANES = 8
MESH = pl.DeviceIdType.MESH
BF16, F32, I32 = jnp.bfloat16, jnp.float32, jnp.int32


def lane_pick(table, lanes):
    return jnp.take_along_axis(table, lanes, axis=1, mode="promise_in_bounds")


def feature_tile(x_ref, idx_ref, start):
    steps, residues = x_ref.shape[1:]
    groups = [(c, t) for c in range(3) for t in range(0, steps, SUBLANES)]
    lanes, chunks = [], []
    for side in range(2):
        index = jnp.broadcast_to(idx_ref[side : side + 1, pl.ds(start, LANES)], (SUBLANES, LANES))
        lanes.append(lax.bitwise_and(index, LANES - 1))
        chunks.append(lax.shift_right_logical(index, 7))
    picked = [[None] * len(groups) for _ in range(2)]
    for chunk in range(residues // LANES):
        masks = [chunks[side] == chunk for side in range(2)]
        for g, (c, t) in enumerate(groups):
            table = x_ref[c, t : t + SUBLANES, chunk * LANES : (chunk + 1) * LANES]
            for side in range(2):
                found = lane_pick(table, lanes[side])
                old = picked[side][g]
                picked[side][g] = found if old is None else jnp.where(masks[side], found, old)
    halves = steps // SUBLANES
    out = []
    for h in range(halves):
        total = None
        for c in range(3):
            g = c * halves + h
            diff = picked[0][g] - picked[1][g]
            total = diff * diff if total is None else total + diff * diff
        out.append(1.0 / jnp.maximum(jnp.sqrt(total), DIST_FLOOR))
    return jnp.concatenate(out, axis=0).astype(BF16)


def feature_kernel(x_ref, idx_ref, out_ref):
    blocks, _, width = out_ref.shape
    tiles = width // LANES

    def tile(q, carry):
        b, within = q // tiles, (q % tiles) * LANES
        start = pl.multiple_of(q * LANES, LANES)
        out_ref[b, :, pl.ds(pl.multiple_of(within, LANES), LANES)] = feature_tile(x_ref, idx_ref, start)
        return carry

    lax.fori_loop(0, blocks * tiles, tile, 0)


def exchange_kernel(n, n_rep, feat_ref, swap_ref, rows_ref, cols_ref, swaps_ref,
                    s_row1, r_row1, s_col1, r_col1, s_row2, r_row2, s_col2, r_col2, s_sw, r_sw, own_sem):
    i0 = lax.axis_index("tm")
    g0 = lax.axis_index("feat") * n_rep + lax.axis_index("rep")
    is_lead = i0 < n - 1

    def time_id(i):
        return {"tm": i}

    def group_id(j):
        return {"feat": j // n_rep, "rep": j % n_rep}

    def others(me, body):
        def step(d, carry):
            body((me + d) % n)
            return carry
        lax.fori_loop(1, n, step, 0)

    def remote(src, dst, send, recv, device):
        return pltpu.make_async_remote_copy(
            src_ref=src, dst_ref=dst, send_sem=send, recv_sem=recv, device_id=device, device_id_type=MESH)

    def row1(i):
        return remote(feat_ref.at[i], rows_ref.at[i0, g0], s_row1.at[i], r_row1.at[i0], time_id(i))

    def row1_in(i):
        return remote(feat_ref.at[i0], rows_ref.at[i, g0], s_row1.at[i], r_row1.at[i], time_id(i))

    def col1(j):
        return remote(feat_ref.at[j], cols_ref.at[i0, g0], s_col1.at[j], r_col1.at[g0], group_id(j))

    def col1_in(j):
        return remote(feat_ref.at[g0], cols_ref.at[i0, j], s_col1.at[j], r_col1.at[j], group_id(j))

    def row2(i, j):
        return remote(rows_ref.at[i, g0], rows_ref.at[i, g0], s_row2.at[i, j], r_row2.at[i, g0], group_id(j))

    def row2_in(i, j):
        return remote(rows_ref.at[i, j], rows_ref.at[i, j], s_row2.at[i, j], r_row2.at[i, j], group_id(j))

    def col2(i, j):
        return remote(cols_ref.at[i0, j], cols_ref.at[i0, j], s_col2.at[i, j], r_col2.at[i0, j], time_id(i))

    def col2_in(i, j):
        return remote(cols_ref.at[i, j], cols_ref.at[i, j], s_col2.at[i, j], r_col2.at[i, j], time_id(i))

    def swap(i):
        return remote(swap_ref, swaps_ref.at[i0], s_sw.at[i], r_sw.at[i0], time_id(i))

    def swap_in(i):
        return remote(swap_ref, swaps_ref.at[i], s_sw.at[i], r_sw.at[i], time_id(i))

    barrier = pltpu.get_barrier_semaphore()
    others(i0, lambda i: pl.semaphore_signal(barrier, inc=1, device_id=time_id(i), device_id_type=MESH))
    others(g0, lambda j: pl.semaphore_signal(barrier, inc=1, device_id=group_id(j), device_id_type=MESH))
    pl.semaphore_wait(barrier, 2 * (n - 1))

    others(g0, lambda j: col1(j).start())

    @pl.when(is_lead)
    def _():
        others(i0, lambda i: row1(i).start())

    own_col = pltpu.make_async_copy(feat_ref.at[g0], cols_ref.at[i0, g0], own_sem.at[0])
    own_sw = pltpu.make_async_copy(swap_ref, swaps_ref.at[i0], own_sem.at[2])
    own_col.start()
    own_sw.start()
    others(i0, lambda i: swap(i).start())

    @pl.when(is_lead)
    def _():
        own_row = pltpu.make_async_copy(feat_ref.at[i0], rows_ref.at[i0, g0], own_sem.at[1])
        own_row.start()
        own_row.wait()
        others(g0, lambda j: row2(i0, j).start())

    own_col.wait()
    others(i0, lambda i: col2(i, g0).start())

    def forward_col(j):
        col1_in(j).wait_recv()
        others(i0, lambda i: col2(i, j).start())

    others(g0, forward_col)

    def forward_row(i):
        @pl.when(i < n - 1)
        def _():
            row1_in(i).wait_recv()
            others(g0, lambda j: row2(i, j).start())

    others(i0, forward_row)

    own_sw.wait()

    def finish_swap(i):
        swap_in(i).wait_recv()
        swap(i).wait_send()

    others(i0, finish_swap)
    others(g0, lambda j: col1(j).wait_send())

    @pl.when(is_lead)
    def _():
        others(i0, lambda i: row1(i).wait_send())

    def end_rows(i, carry):
        def one(j):
            row2(i, j).wait_send()
            row2_in(i, j).wait_recv()
        others(g0, one)
        return carry

    lax.fori_loop(0, n - 1, end_rows, 0)

    def end_cols(j, carry):
        def one(i):
            col2(i, j).wait_send()
            col2_in(i, j).wait_recv()
        others(i0, one)
        return carry

    lax.fori_loop(0, n, end_cols, 0)


def covariance_kernel(frames, rows_ref, cols_ref, swaps_ref, inst_ref, lag_ref, lagged_ref, means_ref):
    blocks, per, _ = cols_ref.shape
    lead_rows = (blocks - 1) * per
    kept = lead_rows
    scale = 1.0 / frames

    @pl.when(pl.program_id(0) == 0)
    def _():
        here = lax.broadcasted_iota(I32, (per, per), 0) % LAG
        there = lax.broadcasted_iota(I32, (per, per), 1) % LAG
        same_step = here == there
        for i in range(blocks - 1):
            now = jnp.broadcast_to(swaps_ref[i, 0:1, :], (per, per)).T
            later = jnp.broadcast_to(swaps_ref[i + 1, 0:1, :], (per, per))
            pairs = jnp.where(same_step & (now == later), 1.0, 0.0).astype(BF16)
            lagged_ref[i * per : (i + 1) * per, :] = jnp.dot(
                pairs, cols_ref[i + 1], preferred_element_type=F32).astype(BF16)
        ones = jnp.ones((SUBLANES, kept), BF16)
        lead = cols_ref[: blocks - 1].reshape(kept, cols_ref.shape[2])
        means_ref[0] = jnp.dot(ones, lead, preferred_element_type=F32) * scale
        means_ref[1] = jnp.dot(ones, lagged_ref[...], preferred_element_type=F32) * scale

    rows = rows_ref[...].reshape(kept, rows_ref.shape[2])
    lead = cols_ref[: blocks - 1].reshape(kept, cols_ref.shape[2])
    contract = (((0,), (0,)), ((), ()))
    row_mean = lax.dot_general(rows, jnp.ones((kept, LANES), BF16), contract, preferred_element_type=F32)
    row_mean = row_mean[:, :1] * scale
    inst = lax.dot_general(rows, lead, contract, preferred_element_type=F32)
    inst_ref[...] = inst * scale - row_mean * means_ref[0, 0:1, :]
    lag = lax.dot_general(rows, lagged_ref[...], contract, preferred_element_type=F32)
    lag_ref[...] = lag * scale - row_mean * means_ref[1, 0:1, :]


def vmem(count):
    return [pl.BlockSpec(memory_space=pltpu.VMEM)] * count


def solution(mesh):
    n = mesh.shape["tm"]
    n_rep = mesh.shape["rep"]

    def local(archive, swap_history, pair_index):
        steps, _, _, residues = archive.shape
        feats = pair_index.shape[1]
        width = feats // n
        per = n * steps
        x = jnp.swapaxes(archive[:, 0], 0, 1)
        swap = jnp.broadcast_to(swap_history.T.reshape(1, per).astype(F32), (SUBLANES, per))
        features = pl.pallas_call(
            feature_kernel,
            out_shape=jax.ShapeDtypeStruct((n, steps, width), BF16),
            in_specs=vmem(2),
            out_specs=vmem(1)[0],
            compiler_params=pltpu.CompilerParams(vmem_limit_bytes=32 << 20),
        )(x, pair_index)
        dma = pltpu.SemaphoreType.DMA
        rows, cols, swaps = pl.pallas_call(
            functools.partial(exchange_kernel, n, n_rep),
            out_shape=[
                jax.ShapeDtypeStruct((n - 1, n, steps, width), BF16),
                jax.ShapeDtypeStruct((n, n, steps, width), BF16),
                jax.ShapeDtypeStruct((n, SUBLANES, per), F32),
            ],
            in_specs=vmem(2),
            out_specs=vmem(3),
            scratch_shapes=[dma((n,)), dma((n,)), dma((n,)), dma((n,)),
                            dma((n, n)), dma((n, n)), dma((n, n)), dma((n, n)),
                            dma((n,)), dma((n,)), dma((3,))],
            compiler_params=pltpu.CompilerParams(
                collective_id=0, has_side_effects=True, vmem_limit_bytes=32 << 20),
        )(features, swap)
        tile = min(256, width)
        shape = jax.ShapeDtypeStruct((width, width), F32)
        return pl.pallas_call(
            functools.partial(covariance_kernel, (n - 1) * per),
            grid=(width // tile,),
            out_shape=[shape, shape],
            in_specs=[
                pl.BlockSpec((n - 1, per, tile), lambda r: (0, 0, r)),
                pl.BlockSpec((n, per, width), lambda r: (0, 0, 0)),
                pl.BlockSpec((n, SUBLANES, per), lambda r: (0, 0, 0)),
            ],
            out_specs=[pl.BlockSpec((tile, width), lambda r: (r, 0))] * 2,
            scratch_shapes=[pltpu.VMEM(((n - 1) * per, width), BF16), pltpu.VMEM((2, SUBLANES, width), F32)],
            compiler_params=pltpu.CompilerParams(vmem_limit_bytes=48 << 20),
        )(rows.reshape(n - 1, per, width), cols.reshape(n, per, width), swaps)

    return jax.shard_map(
        local,
        mesh=mesh,
        in_specs=(P(("grp", "tm"), ("feat", "rep"), None, None), P(("grp", "tm"), None), P()),
        out_specs=(P(("grp", "tm"), ("feat", "rep")), P(("grp", "tm"), ("feat", "rep"))),
        check_vma=False,
    )
```

```python
import functools

import jax
import jax.numpy as jnp
from jax import lax
from jax.experimental import pallas as pl
from jax.experimental.pallas import tpu as pltpu
from jax.sharding import PartitionSpec as P

LAG = 16
DIST_FLOOR = 0.3
LANES = 128
SUBLANES = 8
MESH = pl.DeviceIdType.MESH
BF16, F32, I32 = jnp.bfloat16, jnp.float32, jnp.int32


def lane_pick(table, lanes):
    return jnp.take_along_axis(table, lanes, axis=1, mode="promise_in_bounds")


def feature_tile(x_ref, idx_ref, start):
    steps, residues = x_ref.shape[1:]
    groups = [(c, t) for c in range(3) for t in range(0, steps, SUBLANES)]
    lanes, chunks = [], []
    for side in range(2):
        index = jnp.broadcast_to(idx_ref[side : side + 1, pl.ds(start, LANES)], (SUBLANES, LANES))
        lanes.append(lax.bitwise_and(index, LANES - 1))
        chunks.append(lax.shift_right_logical(index, 7))
    picked = [[None] * len(groups) for _ in range(2)]
    for chunk in range(residues // LANES):
        masks = [chunks[side] == chunk for side in range(2)]
        for g, (c, t) in enumerate(groups):
            table = x_ref[c, t : t + SUBLANES, chunk * LANES : (chunk + 1) * LANES]
            for side in range(2):
                found = lane_pick(table, lanes[side])
                old = picked[side][g]
                picked[side][g] = found if old is None else jnp.where(masks[side], found, old)
    halves = steps // SUBLANES
    out = []
    for h in range(halves):
        total = None
        for c in range(3):
            g = c * halves + h
            diff = picked[0][g] - picked[1][g]
            total = diff * diff if total is None else total + diff * diff
        out.append(1.0 / jnp.maximum(jnp.sqrt(total), DIST_FLOOR))
    return jnp.concatenate(out, axis=0).astype(BF16)


def flat_swaps(swap):
    states, steps = swap.shape
    per = steps * states
    lane = lax.broadcasted_iota(I32, (steps, per), 1)
    spread = jnp.where(lane % steps == lax.broadcasted_iota(I32, (steps, per), 0), 1.0, 0.0)
    wide = jnp.dot(swap.astype(F32).astype(BF16), spread.astype(BF16), preferred_element_type=F32)
    lane = lax.broadcasted_iota(I32, (states, per), 1)
    mine = lane // steps == lax.broadcasted_iota(I32, (states, per), 0)
    row = jnp.sum(jnp.where(mine, wide, 0.0), axis=0, keepdims=True)
    return jnp.broadcast_to(row, (SUBLANES, per))


def exchange_kernel(n, n_rep, raw_ref, idx_hbm, swap_in_ref, rows_ref, cols_ref, swaps_ref,
                    raw, idx_ref, x_ref, feat_ref, swap_ref,
                    s_row1, r_row1, s_col1, r_col1, s_row2, r_row2, s_col2, r_col2, s_sw, r_sw, own_sem):
    i0 = lax.axis_index("tm")
    g0 = lax.axis_index("feat") * n_rep + lax.axis_index("rep")
    is_lead = i0 < n - 1
    get_raw = pltpu.make_async_copy(raw_ref, raw, own_sem.at[0])
    get_idx = pltpu.make_async_copy(idx_hbm, idx_ref, own_sem.at[1])
    get_raw.start()
    get_idx.start()

    def time_id(i):
        return {"tm": i}

    def group_id(j):
        return {"feat": j // n_rep, "rep": j % n_rep}

    def others(me, body):
        def step(d, carry):
            body((me + d) % n)
            return carry
        lax.fori_loop(1, n, step, 0)

    def remote(src, dst, send, recv, device):
        return pltpu.make_async_remote_copy(
            src_ref=src, dst_ref=dst, send_sem=send, recv_sem=recv, device_id=device, device_id_type=MESH)

    def row1(i):
        return remote(feat_ref.at[i], rows_ref.at[i0, g0], s_row1.at[i], r_row1.at[i0], time_id(i))

    def row1_in(i):
        return remote(feat_ref.at[i0], rows_ref.at[i, g0], s_row1.at[i], r_row1.at[i], time_id(i))

    def col1(j):
        return remote(feat_ref.at[j], cols_ref.at[i0, g0], s_col1.at[j], r_col1.at[g0], group_id(j))

    def col1_in(j):
        return remote(feat_ref.at[g0], cols_ref.at[i0, j], s_col1.at[j], r_col1.at[j], group_id(j))

    def row2(i, j):
        return remote(rows_ref.at[i, g0], rows_ref.at[i, g0], s_row2.at[i, j], r_row2.at[i, g0], group_id(j))

    def row2_in(i, j):
        return remote(rows_ref.at[i, j], rows_ref.at[i, j], s_row2.at[i, j], r_row2.at[i, j], group_id(j))

    def col2(i, j):
        return remote(cols_ref.at[i0, j], cols_ref.at[i0, j], s_col2.at[i, j], r_col2.at[i0, j], time_id(i))

    def col2_in(i, j):
        return remote(cols_ref.at[i, j], cols_ref.at[i, j], s_col2.at[i, j], r_col2.at[i, j], time_id(i))

    def swap(i):
        return remote(swap_ref, swaps_ref.at[i0], s_sw.at[i], r_sw.at[i0], time_id(i))

    def swap_in(i):
        return remote(swap_ref, swaps_ref.at[i], s_sw.at[i], r_sw.at[i], time_id(i))

    barrier = pltpu.get_barrier_semaphore()
    others(i0, lambda i: pl.semaphore_signal(barrier, inc=1, device_id=time_id(i), device_id_type=MESH))
    others(g0, lambda j: pl.semaphore_signal(barrier, inc=1, device_id=group_id(j), device_id_type=MESH))

    swap_ref[...] = flat_swaps(swap_in_ref[...])
    swaps_ref[i0] = swap_ref[...]
    _, steps, residues = x_ref.shape
    chunks = residues // LANES
    width = feat_ref.shape[2]
    get_raw.wait()
    for c in range(3):
        for t in range(0, steps, SUBLANES):
            for h in range(chunks):
                x_ref[c, t : t + SUBLANES, h * LANES : (h + 1) * LANES] = raw[
                    pl.ds((t * 3 + c) * chunks + h, SUBLANES, stride=3 * chunks), :]
    get_idx.wait()
    pl.semaphore_wait(barrier, 2 * (n - 1))
    others(i0, lambda i: swap(i).start())

    def forward(k):
        j = (g0 - i0 - k + 2 * n) % n
        i = (i0 - g0 - k + 2 * n) % n

        @pl.when(j != g0)
        def _():
            col1_in(j).wait_recv()
            others(i0, lambda to: col2(to, j).start())

        @pl.when((i != i0) & (i < n - 1))
        def _():
            row1_in(i).wait_recv()
            others(g0, lambda to: row2(i, to).start())

    def block(k, carry):
        b = (i0 + g0 + k) % n

        def tile(q, carry):
            start = pl.multiple_of(b * width + q * LANES, LANES)
            feat_ref[b, :, pl.ds(pl.multiple_of(q * LANES, LANES), LANES)] = feature_tile(x_ref, idx_ref, start)
            return carry

        lax.fori_loop(0, width // LANES, tile, 0)

        @pl.when(b != g0)
        def _():
            col1(b).start()

        @pl.when((b != i0) & is_lead)
        def _():
            row1(b).start()

        @pl.when(b == g0)
        def _():
            cols_ref[i0, g0] = feat_ref[b]
            others(i0, lambda to: col2(to, g0).start())

        @pl.when((b == i0) & is_lead)
        def _():
            rows_ref[i0, g0] = feat_ref[b]
            others(g0, lambda to: row2(i0, to).start())

        @pl.when(k > 0)
        def _():
            forward(k - 1)

        return carry

    lax.fori_loop(0, n, block, 0)
    forward(n - 1)

    def finish_swap(i):
        swap_in(i).wait_recv()
        swap(i).wait_send()

    others(i0, finish_swap)
    others(g0, lambda j: col1(j).wait_send())

    @pl.when(is_lead)
    def _():
        others(i0, lambda i: row1(i).wait_send())

    def end_rows(i, carry):
        def one(j):
            row2(i, j).wait_send()
            row2_in(i, j).wait_recv()
        others(g0, one)
        return carry

    lax.fori_loop(0, n - 1, end_rows, 0)

    def end_cols(j, carry):
        def one(i):
            col2(i, j).wait_send()
            col2_in(i, j).wait_recv()
        others(i0, one)
        return carry

    lax.fori_loop(0, n, end_cols, 0)


def covariance_kernel(frames, rows_ref, cols_ref, swaps_ref, inst_ref, lag_ref, lagged_ref, means_ref):
    blocks, per, _ = cols_ref.shape
    lead_rows = (blocks - 1) * per
    kept = lead_rows
    scale = 1.0 / frames

    @pl.when(pl.program_id(0) == 0)
    def _():
        here = lax.broadcasted_iota(I32, (per, per), 0) % LAG
        there = lax.broadcasted_iota(I32, (per, per), 1) % LAG
        same_step = here == there
        for i in range(blocks - 1):
            now = jnp.broadcast_to(swaps_ref[i, 0:1, :], (per, per)).T
            later = jnp.broadcast_to(swaps_ref[i + 1, 0:1, :], (per, per))
            pairs = jnp.where(same_step & (now == later), 1.0, 0.0).astype(BF16)
            lagged_ref[i * per : (i + 1) * per, :] = jnp.dot(
                pairs, cols_ref[i + 1], preferred_element_type=F32).astype(BF16)
        ones = jnp.ones((SUBLANES, kept), BF16)
        lead = cols_ref[: blocks - 1].reshape(kept, cols_ref.shape[2])
        means_ref[0] = jnp.dot(ones, lead, preferred_element_type=F32) * scale
        means_ref[1] = jnp.dot(ones, lagged_ref[...], preferred_element_type=F32) * scale

    rows = rows_ref[...].reshape(kept, rows_ref.shape[2])
    lead = cols_ref[: blocks - 1].reshape(kept, cols_ref.shape[2])
    contract = (((0,), (0,)), ((), ()))
    row_mean = lax.dot_general(rows, jnp.ones((kept, LANES), BF16), contract, preferred_element_type=F32)
    row_mean = row_mean[:, :1] * scale
    inst = lax.dot_general(rows, lead, contract, preferred_element_type=F32)
    inst_ref[...] = inst * scale - row_mean * means_ref[0, 0:1, :]
    lag = lax.dot_general(rows, lagged_ref[...], contract, preferred_element_type=F32)
    lag_ref[...] = lag * scale - row_mean * means_ref[1, 0:1, :]


def vmem(count):
    return [pl.BlockSpec(memory_space=pltpu.VMEM)] * count


def solution(mesh):
    n = mesh.shape["tm"]
    n_rep = mesh.shape["rep"]

    def local(archive, swap_history, pair_index):
        steps, _, _, residues = archive.shape
        feats = pair_index.shape[1]
        width = feats // n
        per = n * steps
        raw = archive.reshape(steps * 3 * residues // LANES, LANES)
        dma = pltpu.SemaphoreType.DMA
        rows, cols, swaps = pl.pallas_call(
            functools.partial(exchange_kernel, n, n_rep),
            out_shape=[
                jax.ShapeDtypeStruct((n - 1, n, steps, width), BF16),
                jax.ShapeDtypeStruct((n, n, steps, width), BF16),
                jax.ShapeDtypeStruct((n, SUBLANES, per), F32),
            ],
            in_specs=[pl.BlockSpec(memory_space=pl.ANY)] * 2 + vmem(1),
            out_specs=vmem(3),
            scratch_shapes=[pltpu.VMEM(raw.shape, F32), pltpu.VMEM(pair_index.shape, I32),
                            pltpu.VMEM((3, steps, residues), F32), pltpu.VMEM((n, steps, width), BF16),
                            pltpu.VMEM((SUBLANES, per), F32),
                            dma((n,)), dma((n,)), dma((n,)), dma((n,)),
                            dma((n, n)), dma((n, n)), dma((n, n)), dma((n, n)),
                            dma((n,)), dma((n,)), dma((2,))],
            compiler_params=pltpu.CompilerParams(
                collective_id=0, has_side_effects=True, vmem_limit_bytes=32 << 20),
        )(raw, pair_index, swap_history.T)
        tile = min(256, width)
        shape = jax.ShapeDtypeStruct((width, width), F32)
        return pl.pallas_call(
            functools.partial(covariance_kernel, (n - 1) * per),
            grid=(width // tile,),
            out_shape=[shape, shape],
            in_specs=[
                pl.BlockSpec((n - 1, per, tile), lambda r: (0, 0, r)),
                pl.BlockSpec((n, per, width), lambda r: (0, 0, 0)),
                pl.BlockSpec((n, SUBLANES, per), lambda r: (0, 0, 0)),
            ],
            out_specs=[pl.BlockSpec((tile, width), lambda r: (r, 0))] * 2,
            scratch_shapes=[pltpu.VMEM(((n - 1) * per, width), BF16), pltpu.VMEM((2, SUBLANES, width), F32)],
            compiler_params=pltpu.CompilerParams(vmem_limit_bytes=48 << 20),
        )(rows.reshape(n - 1, per, width), cols.reshape(n, per, width), swaps)

    return jax.shard_map(
        local,
        mesh=mesh,
        in_specs=(P(("grp", "tm"), ("feat", "rep"), None, None), P(("grp", "tm"), None), P()),
        out_specs=(P(("grp", "tm"), ("feat", "rep")), P(("grp", "tm"), ("feat", "rep"))),
        check_vma=False,
    )
```

```python
import functools

import jax
import jax.numpy as jnp
from jax import lax
from jax.experimental import pallas as pl
from jax.experimental.pallas import tpu as pltpu
from jax.sharding import PartitionSpec as P

LAG = 16
DIST_FLOOR = 0.3
LANES = 128
SUBLANES = 8
DEPTH = 256
BF16_MAX = float(jnp.finfo(jnp.bfloat16).max)
MESH = pl.DeviceIdType.MESH
BF16, F32, I32 = jnp.bfloat16, jnp.float32, jnp.int32


def pieces(value):
    high = jnp.clip(value, -BF16_MAX, BF16_MAX).astype(BF16)
    rest = value - high.astype(F32)
    middle = rest.astype(BF16)
    return high, middle, (rest - middle.astype(F32)).astype(BF16)


def feature_block(parts_ref, idx_ref, start, width, steps):
    count, residues = parts_ref.shape
    one, two = (idx_ref[side : side + 1, pl.ds(start, width)] for side in range(2))
    same = one == two
    one, two = jnp.where(same, -1, one), jnp.where(same, -1, two)
    shape = (DEPTH, width)
    residue = lax.broadcasted_iota(I32, shape, 0).astype(jnp.int16)
    plus, zero = jnp.ones(shape, BF16), jnp.zeros(shape, BF16)
    total = None
    for first in range(0, residues, DEPTH):
        at_one = residue == jnp.broadcast_to(one - first, shape).astype(jnp.int16)
        at_two = residue == jnp.broadcast_to(two - first, shape).astype(jnp.int16)
        chosen = jnp.where(at_one, plus, jnp.where(at_two, -plus, zero))
        part = jnp.dot(parts_ref[:, first : first + DEPTH], chosen, preferred_element_type=F32)
        total = part if total is None else total + part
    third = count // 3
    displace = total[:third] + total[third : 2 * third] + total[2 * third :]
    square = displace * displace
    square = square[:steps] + square[steps : 2 * steps] + square[2 * steps :]
    return (1.0 / jnp.maximum(jnp.sqrt(square), DIST_FLOOR)).astype(BF16)


def flat_swaps(swap):
    states, steps = swap.shape
    per = steps * states
    lane = lax.broadcasted_iota(I32, (steps, per), 1)
    spread = jnp.where(lane % steps == lax.broadcasted_iota(I32, (steps, per), 0), 1.0, 0.0)
    wide = jnp.dot(swap.astype(F32).astype(BF16), spread.astype(BF16), preferred_element_type=F32)
    lane = lax.broadcasted_iota(I32, (states, per), 1)
    mine = lane // steps == lax.broadcasted_iota(I32, (states, per), 0)
    row = jnp.sum(jnp.where(mine, wide, 0.0), axis=0, keepdims=True)
    return jnp.broadcast_to(row, (SUBLANES, per))


def exchange_kernel(n, n_rep, raw_ref, idx_hbm, swap_in_ref, rows_ref, cols_ref, swaps_ref,
                    raw, idx_ref, parts_ref, feat_ref, swap_ref,
                    s_row1, r_row1, s_col1, r_col1, s_row2, r_row2, s_col2, r_col2, s_sw, r_sw, own_sem):
    i0 = lax.axis_index("tm")
    g0 = lax.axis_index("feat") * n_rep + lax.axis_index("rep")
    is_lead = i0 < n - 1
    get_raw = pltpu.make_async_copy(raw_ref, raw, own_sem.at[0])
    get_idx = pltpu.make_async_copy(idx_hbm, idx_ref, own_sem.at[1])
    get_raw.start()
    get_idx.start()

    def time_id(i):
        return {"tm": i}

    def group_id(j):
        return {"feat": j // n_rep, "rep": j % n_rep}

    def others(me, body):
        def step(d, carry):
            body((me + d) % n)
            return carry
        lax.fori_loop(1, n, step, 0)

    def remote(src, dst, send, recv, device):
        return pltpu.make_async_remote_copy(
            src_ref=src, dst_ref=dst, send_sem=send, recv_sem=recv, device_id=device, device_id_type=MESH)

    def row1(i):
        return remote(feat_ref.at[i], rows_ref.at[i0, g0], s_row1.at[i], r_row1.at[i0], time_id(i))

    def row1_in(i):
        return remote(feat_ref.at[i0], rows_ref.at[i, g0], s_row1.at[i], r_row1.at[i], time_id(i))

    def col1(j):
        return remote(feat_ref.at[j], cols_ref.at[i0, g0], s_col1.at[j], r_col1.at[g0], group_id(j))

    def col1_in(j):
        return remote(feat_ref.at[g0], cols_ref.at[i0, j], s_col1.at[j], r_col1.at[j], group_id(j))

    def row2(i, j):
        return remote(rows_ref.at[i, g0], rows_ref.at[i, g0], s_row2.at[i, j], r_row2.at[i, g0], group_id(j))

    def row2_in(i, j):
        return remote(rows_ref.at[i, j], rows_ref.at[i, j], s_row2.at[i, j], r_row2.at[i, j], group_id(j))

    def col2(i, j):
        return remote(cols_ref.at[i0, j], cols_ref.at[i0, j], s_col2.at[i, j], r_col2.at[i0, j], time_id(i))

    def col2_in(i, j):
        return remote(cols_ref.at[i, j], cols_ref.at[i, j], s_col2.at[i, j], r_col2.at[i, j], time_id(i))

    def swap(i):
        return remote(swap_ref, swaps_ref.at[i0], s_sw.at[i], r_sw.at[i0], time_id(i))

    def swap_in(i):
        return remote(swap_ref, swaps_ref.at[i], s_sw.at[i], r_sw.at[i], time_id(i))

    barrier = pltpu.get_barrier_semaphore()
    others(i0, lambda i: pl.semaphore_signal(barrier, inc=1, device_id=time_id(i), device_id_type=MESH))
    others(g0, lambda j: pl.semaphore_signal(barrier, inc=1, device_id=group_id(j), device_id_type=MESH))

    swap_ref[...] = flat_swaps(swap_in_ref[...])
    swaps_ref[i0] = swap_ref[...]
    count, residues = parts_ref.shape
    steps = feat_ref.shape[1]
    chunks = residues // LANES
    width = feat_ref.shape[2]
    get_raw.wait()
    for c in range(3):
        for h in range(chunks):
            rows = [raw[pl.ds((t * 3 + c) * chunks + h, SUBLANES, stride=3 * chunks), :]
                    for t in range(0, steps, SUBLANES)]
            for p, piece in enumerate(pieces(jnp.concatenate(rows, axis=0))):
                top = (p * 3 + c) * steps
                parts_ref[top : top + steps, h * LANES : (h + 1) * LANES] = piece
    get_idx.wait()
    pl.semaphore_wait(barrier, 2 * (n - 1))
    others(i0, lambda i: swap(i).start())

    def forward(k):
        j = (g0 - i0 - k + 2 * n) % n
        i = (i0 - g0 - k + 2 * n) % n

        @pl.when(j != g0)
        def _():
            col1_in(j).wait_recv()
            others(i0, lambda to: col2(to, j).start())

        @pl.when((i != i0) & (i < n - 1))
        def _():
            row1_in(i).wait_recv()
            others(g0, lambda to: row2(i, to).start())

    def block(k, carry):
        b = (i0 + g0 + k) % n

        start = pl.multiple_of(b * width, LANES)
        feat_ref[b] = feature_block(parts_ref, idx_ref, start, width, steps)

        @pl.when(b != g0)
        def _():
            col1(b).start()

        @pl.when((b != i0) & is_lead)
        def _():
            row1(b).start()

        @pl.when(b == g0)
        def _():
            cols_ref[i0, g0] = feat_ref[b]
            others(i0, lambda to: col2(to, g0).start())

        @pl.when((b == i0) & is_lead)
        def _():
            rows_ref[i0, g0] = feat_ref[b]
            others(g0, lambda to: row2(i0, to).start())

        @pl.when(k > 0)
        def _():
            forward(k - 1)

        return carry

    lax.fori_loop(0, n, block, 0)
    forward(n - 1)

    def finish_swap(i):
        swap_in(i).wait_recv()
        swap(i).wait_send()

    others(i0, finish_swap)
    others(g0, lambda j: col1(j).wait_send())

    @pl.when(is_lead)
    def _():
        others(i0, lambda i: row1(i).wait_send())

    def end_rows(i, carry):
        def one(j):
            row2(i, j).wait_send()
            row2_in(i, j).wait_recv()
        others(g0, one)
        return carry

    lax.fori_loop(0, n - 1, end_rows, 0)

    def end_cols(j, carry):
        def one(i):
            col2(i, j).wait_send()
            col2_in(i, j).wait_recv()
        others(i0, one)
        return carry

    lax.fori_loop(0, n, end_cols, 0)


def covariance_kernel(frames, rows_ref, cols_ref, swaps_ref, inst_ref, lag_ref, lagged_ref, means_ref):
    blocks, per, _ = cols_ref.shape
    lead_rows = (blocks - 1) * per
    kept = lead_rows
    scale = 1.0 / frames

    @pl.when(pl.program_id(0) == 0)
    def _():
        here = lax.broadcasted_iota(I32, (per, per), 0) % LAG
        there = lax.broadcasted_iota(I32, (per, per), 1) % LAG
        same_step = here == there
        for i in range(blocks - 1):
            now = jnp.broadcast_to(swaps_ref[i, 0:1, :], (per, per)).T
            later = jnp.broadcast_to(swaps_ref[i + 1, 0:1, :], (per, per))
            pairs = jnp.where(same_step & (now == later), 1.0, 0.0).astype(BF16)
            lagged_ref[i * per : (i + 1) * per, :] = jnp.dot(
                pairs, cols_ref[i + 1], preferred_element_type=F32).astype(BF16)
        ones = jnp.ones((SUBLANES, kept), BF16)
        lead = cols_ref[: blocks - 1].reshape(kept, cols_ref.shape[2])
        means_ref[0] = jnp.dot(ones, lead, preferred_element_type=F32) * scale
        means_ref[1] = jnp.dot(ones, lagged_ref[...], preferred_element_type=F32) * scale

    rows = rows_ref[...].reshape(kept, rows_ref.shape[2])
    lead = cols_ref[: blocks - 1].reshape(kept, cols_ref.shape[2])
    contract = (((0,), (0,)), ((), ()))
    row_mean = lax.dot_general(rows, jnp.ones((kept, LANES), BF16), contract, preferred_element_type=F32)
    row_mean = row_mean[:, :1] * scale
    inst = lax.dot_general(rows, lead, contract, preferred_element_type=F32)
    inst_ref[...] = inst * scale - row_mean * means_ref[0, 0:1, :]
    lag = lax.dot_general(rows, lagged_ref[...], contract, preferred_element_type=F32)
    lag_ref[...] = lag * scale - row_mean * means_ref[1, 0:1, :]


def vmem(count):
    return [pl.BlockSpec(memory_space=pltpu.VMEM)] * count


def solution(mesh):
    n = mesh.shape["tm"]
    n_rep = mesh.shape["rep"]

    def local(archive, swap_history, pair_index):
        steps, _, _, residues = archive.shape
        feats = pair_index.shape[1]
        width = feats // n
        per = n * steps
        raw = archive.reshape(steps * 3 * residues // LANES, LANES)
        dma = pltpu.SemaphoreType.DMA
        rows, cols, swaps = pl.pallas_call(
            functools.partial(exchange_kernel, n, n_rep),
            out_shape=[
                jax.ShapeDtypeStruct((n - 1, n, steps, width), BF16),
                jax.ShapeDtypeStruct((n, n, steps, width), BF16),
                jax.ShapeDtypeStruct((n, SUBLANES, per), F32),
            ],
            in_specs=[pl.BlockSpec(memory_space=pl.ANY)] * 2 + vmem(1),
            out_specs=vmem(3),
            scratch_shapes=[pltpu.VMEM(raw.shape, F32), pltpu.VMEM(pair_index.shape, I32),
                            pltpu.VMEM((9 * steps, residues), BF16), pltpu.VMEM((n, steps, width), BF16),
                            pltpu.VMEM((SUBLANES, per), F32),
                            dma((n,)), dma((n,)), dma((n,)), dma((n,)),
                            dma((n, n)), dma((n, n)), dma((n, n)), dma((n, n)),
                            dma((n,)), dma((n,)), dma((2,))],
            compiler_params=pltpu.CompilerParams(
                collective_id=0, has_side_effects=True, vmem_limit_bytes=32 << 20),
        )(raw, pair_index, swap_history.T)
        tile = min(256, width)
        shape = jax.ShapeDtypeStruct((width, width), F32)
        return pl.pallas_call(
            functools.partial(covariance_kernel, (n - 1) * per),
            grid=(width // tile,),
            out_shape=[shape, shape],
            in_specs=[
                pl.BlockSpec((n - 1, per, tile), lambda r: (0, 0, r)),
                pl.BlockSpec((n, per, width), lambda r: (0, 0, 0)),
                pl.BlockSpec((n, SUBLANES, per), lambda r: (0, 0, 0)),
            ],
            out_specs=[pl.BlockSpec((tile, width), lambda r: (r, 0))] * 2,
            scratch_shapes=[pltpu.VMEM(((n - 1) * per, width), BF16), pltpu.VMEM((2, SUBLANES, width), F32)],
            compiler_params=pltpu.CompilerParams(vmem_limit_bytes=48 << 20),
        )(rows.reshape(n - 1, per, width), cols.reshape(n, per, width), swaps)

    return jax.shard_map(
        local,
        mesh=mesh,
        in_specs=(P(("grp", "tm"), ("feat", "rep"), None, None), P(("grp", "tm"), None), P()),
        out_specs=(P(("grp", "tm"), ("feat", "rep")), P(("grp", "tm"), ("feat", "rep"))),
        check_vma=False,
    )
```

```python
import functools

import jax
import jax.numpy as jnp
from jax import lax
from jax.experimental import pallas as pl
from jax.experimental.pallas import tpu as pltpu
from jax.sharding import PartitionSpec as P

LAG = 16
DIST_FLOOR = 0.3
LANES = 128
SUBLANES = 8
DEPTH = 256
BF16_MAX = float(jnp.finfo(jnp.bfloat16).max)
MESH = pl.DeviceIdType.MESH
BF16, F32, I32 = jnp.bfloat16, jnp.float32, jnp.int32


def pieces(value):
    high = jnp.clip(value, -BF16_MAX, BF16_MAX).astype(BF16)
    rest = value - high.astype(F32)
    middle = rest.astype(BF16)
    return high, middle, (rest - middle.astype(F32)).astype(BF16)


def feature_block(parts_ref, idx_ref, start, width, steps):
    count, residues = parts_ref.shape
    one, two = (idx_ref[side : side + 1, pl.ds(start, width)] for side in range(2))
    same = one == two
    one, two = jnp.where(same, -1, one), jnp.where(same, -1, two)
    shape = (DEPTH, width)
    residue = lax.broadcasted_iota(I32, shape, 0).astype(jnp.int16)
    plus, zero = jnp.ones(shape, BF16), jnp.zeros(shape, BF16)
    total = None
    for first in range(0, residues, DEPTH):
        at_one = residue == jnp.broadcast_to(one - first, shape).astype(jnp.int16)
        at_two = residue == jnp.broadcast_to(two - first, shape).astype(jnp.int16)
        chosen = jnp.where(at_one, plus, jnp.where(at_two, -plus, zero))
        part = jnp.dot(parts_ref[:, first : first + DEPTH], chosen, preferred_element_type=F32)
        total = part if total is None else total + part
    third = count // 3
    displace = total[:third] + total[third : 2 * third] + total[2 * third :]
    square = displace * displace
    square = square[:steps] + square[steps : 2 * steps] + square[2 * steps :]
    return (1.0 / jnp.maximum(jnp.sqrt(square), DIST_FLOOR)).astype(BF16)


def flat_swaps(swap):
    states, steps = swap.shape
    per = steps * states
    lane = lax.broadcasted_iota(I32, (steps, per), 1)
    spread = jnp.where(lane % steps == lax.broadcasted_iota(I32, (steps, per), 0), 1.0, 0.0)
    wide = jnp.dot(swap.astype(F32).astype(BF16), spread.astype(BF16), preferred_element_type=F32)
    lane = lax.broadcasted_iota(I32, (states, per), 1)
    mine = lane // steps == lax.broadcasted_iota(I32, (states, per), 0)
    row = jnp.sum(jnp.where(mine, wide, 0.0), axis=0, keepdims=True)
    return jnp.broadcast_to(row, (SUBLANES, per))


def exchange_kernel(n, n_rep, raw_hbm, idx_hbm, swap_hbm, rows_ref, cols_ref, swaps_ref,
                    raw, idx_ref, own_swap_ref, parts_ref, feat_ref, swap_ref,
                    s_row1, r_row1, s_col1, r_col1, s_row2, r_row2, s_up, s_down, r_col2, s_sw, r_sw, own_sem):
    i0 = lax.axis_index("tm")
    g0 = lax.axis_index("feat") * n_rep + lax.axis_index("rep")
    is_lead = i0 < n - 1
    get_raw = pltpu.make_async_copy(raw_hbm, raw, own_sem.at[0])
    get_idx = pltpu.make_async_copy(idx_hbm, idx_ref, own_sem.at[1])
    get_raw.start()
    get_idx.start()
    get_swap = pltpu.make_async_copy(swap_hbm, own_swap_ref, own_sem.at[2])
    get_swap.start()

    def time_id(i):
        return {"tm": i}

    def group_id(j):
        return {"feat": j // n_rep, "rep": j % n_rep}

    def others(me, body):
        def step(d, carry):
            body((me + d) % n)
            return carry
        lax.fori_loop(1, n, step, 0)

    def remote(src, dst, send, recv, device):
        return pltpu.make_async_remote_copy(
            src_ref=src, dst_ref=dst, send_sem=send, recv_sem=recv, device_id=device, device_id_type=MESH)

    def row1(i):
        return remote(feat_ref.at[i], rows_ref.at[i0, g0], s_row1.at[i], r_row1.at[i0], time_id(i))

    def row1_in(i):
        return remote(feat_ref.at[i0], rows_ref.at[i, g0], s_row1.at[i], r_row1.at[i], time_id(i))

    def col1(j):
        return remote(feat_ref.at[j], cols_ref.at[i0, g0], s_col1.at[j], r_col1.at[g0], group_id(j))

    def col1_in(j):
        return remote(feat_ref.at[g0], cols_ref.at[i0, j], s_col1.at[j], r_col1.at[j], group_id(j))

    def row2(i, j):
        return remote(rows_ref.at[i, g0], rows_ref.at[i, g0], s_row2.at[i, j], r_row2.at[i, g0], group_id(j))

    def row2_in(i, j):
        return remote(rows_ref.at[i, j], rows_ref.at[i, j], s_row2.at[i, j], r_row2.at[i, j], group_id(j))

    def up(i, j):
        return remote(cols_ref.at[i, j], cols_ref.at[i, j], s_up.at[i, j], r_col2.at[i, j], time_id(i0 + 1))

    def down(i, j):
        return remote(cols_ref.at[i, j], cols_ref.at[i, j], s_down.at[i, j], r_col2.at[i, j], time_id(i0 - 1))

    def col2_in(i, j):
        return remote(cols_ref.at[i, j], cols_ref.at[i, j], s_up.at[i, j], r_col2.at[i, j], time_id(i))

    def spread(j):
        @pl.when(i0 < n - 1)
        def _():
            up(i0, j).start()

        @pl.when(i0 > 0)
        def _():
            down(i0, j).start()

    def relay(k, hop):
        below, above = i0 - hop, i0 + hop

        @pl.when((below >= 0) & (i0 < n - 1))
        def _():
            j = (g0 - below - k + 2 * n) % n
            col2_in(below, j).wait_recv()
            up(below, j).start()

        @pl.when((above < n) & (i0 > 0))
        def _():
            j = (g0 - above - k + 2 * n) % n
            col2_in(above, j).wait_recv()
            down(above, j).start()

    def swap(i):
        return remote(swap_ref, swaps_ref.at[i0], s_sw.at[i], r_sw.at[i0], time_id(i))

    def swap_in(i):
        return remote(swap_ref, swaps_ref.at[i], s_sw.at[i], r_sw.at[i], time_id(i))

    barrier = pltpu.get_barrier_semaphore()
    others(i0, lambda i: pl.semaphore_signal(barrier, inc=1, device_id=time_id(i), device_id_type=MESH))
    others(g0, lambda j: pl.semaphore_signal(barrier, inc=1, device_id=group_id(j), device_id_type=MESH))

    get_swap.wait()
    swap_ref[...] = flat_swaps(own_swap_ref[...])
    swaps_ref[i0] = swap_ref[...]
    count, residues = parts_ref.shape
    steps = feat_ref.shape[1]
    chunks = residues // LANES
    width = feat_ref.shape[2]
    get_raw.wait()
    for c in range(3):
        for h in range(chunks):
            rows = [raw[pl.ds((t * 3 + c) * chunks + h, SUBLANES, stride=3 * chunks), :]
                    for t in range(0, steps, SUBLANES)]
            for p, piece in enumerate(pieces(jnp.concatenate(rows, axis=0))):
                top = (p * 3 + c) * steps
                parts_ref[top : top + steps, h * LANES : (h + 1) * LANES] = piece
    get_idx.wait()
    pl.semaphore_wait(barrier, 2 * (n - 1))
    others(i0, lambda i: swap(i).start())

    def forward(k):
        j = (g0 - i0 - k + 2 * n) % n
        i = (i0 - g0 - k + 2 * n) % n

        @pl.when(j != g0)
        def _():
            col1_in(j).wait_recv()
            spread(j)

        @pl.when((i != i0) & (i < n - 1))
        def _():
            row1_in(i).wait_recv()
            others(g0, lambda to: row2(i, to).start())

    def block(k, carry):
        b = (i0 + g0 + k) % n

        start = pl.multiple_of(b * width, LANES)
        feat_ref[b] = feature_block(parts_ref, idx_ref, start, width, steps)

        @pl.when(b != g0)
        def _():
            col1(b).start()

        @pl.when((b != i0) & is_lead)
        def _():
            row1(b).start()

        @pl.when(b == g0)
        def _():
            cols_ref[i0, g0] = feat_ref[b]
            spread(g0)

        @pl.when((b == i0) & is_lead)
        def _():
            rows_ref[i0, g0] = feat_ref[b]
            others(g0, lambda to: row2(i0, to).start())

        @pl.when(k > 0)
        def _():
            forward(k - 1)

        def relays(hop, carry):
            @pl.when(k - 1 - hop >= 0)
            def _():
                relay(k - 1 - hop, hop)
            return carry

        lax.fori_loop(1, n - 1, relays, 0)
        return carry

    lax.fori_loop(0, n, block, 0)
    forward(n - 1)

    def late(k, carry):
        def relays(hop, carry):
            @pl.when((k - 1 - hop >= 0) & (k - 1 - hop < n))
            def _():
                relay(k - 1 - hop, hop)
            return carry

        lax.fori_loop(1, n - 1, relays, 0)
        return carry

    lax.fori_loop(n, 2 * n - 1, late, 0)

    def finish_swap(i):
        swap_in(i).wait_recv()
        swap(i).wait_send()

    others(i0, finish_swap)
    others(g0, lambda j: col1(j).wait_send())

    @pl.when(is_lead)
    def _():
        others(i0, lambda i: row1(i).wait_send())

    def end_rows(i, carry):
        def one(j):
            row2(i, j).wait_send()
            row2_in(i, j).wait_recv()
        others(g0, one)
        return carry

    lax.fori_loop(0, n - 1, end_rows, 0)

    def end_cols(j, carry):
        def end(i, carry):
            @pl.when((i <= i0) & (i0 < n - 1))
            def _():
                up(i, j).wait_send()

            @pl.when((i >= i0) & (i0 > 0))
            def _():
                down(i, j).wait_send()

            @pl.when(((i < i0) & (i0 == n - 1)) | ((i > i0) & (i0 == 0)))
            def _():
                col2_in(i, j).wait_recv()
            return carry

        lax.fori_loop(0, n, end, 0)
        return carry

    lax.fori_loop(0, n, end_cols, 0)


def covariance_kernel(frames, rows_ref, cols_ref, swaps_ref, inst_ref, lag_ref, lagged_ref, means_ref):
    blocks, per, _ = cols_ref.shape
    lead_rows = (blocks - 1) * per
    kept = lead_rows
    scale = 1.0 / frames

    @pl.when(pl.program_id(0) == 0)
    def _():
        here = lax.broadcasted_iota(I32, (per, per), 0) % LAG
        there = lax.broadcasted_iota(I32, (per, per), 1) % LAG
        same_step = here == there
        for i in range(blocks - 1):
            now = jnp.broadcast_to(swaps_ref[i, 0:1, :], (per, per)).T
            later = jnp.broadcast_to(swaps_ref[i + 1, 0:1, :], (per, per))
            pairs = jnp.where(same_step & (now == later), 1.0, 0.0).astype(BF16)
            lagged_ref[i * per : (i + 1) * per, :] = jnp.dot(
                pairs, cols_ref[i + 1], preferred_element_type=F32).astype(BF16)
        ones = jnp.ones((SUBLANES, kept), BF16)
        lead = cols_ref[: blocks - 1].reshape(kept, cols_ref.shape[2])
        means_ref[0] = jnp.dot(ones, lead, preferred_element_type=F32) * scale
        means_ref[1] = jnp.dot(ones, lagged_ref[...], preferred_element_type=F32) * scale

    rows = rows_ref[...].reshape(kept, rows_ref.shape[2])
    lead = cols_ref[: blocks - 1].reshape(kept, cols_ref.shape[2])
    contract = (((0,), (0,)), ((), ()))
    row_mean = lax.dot_general(rows, jnp.ones((kept, LANES), BF16), contract, preferred_element_type=F32)
    row_mean = row_mean[:, :1] * scale
    inst = lax.dot_general(rows, lead, contract, preferred_element_type=F32)
    inst_ref[...] = inst * scale - row_mean * means_ref[0, 0:1, :]
    lag = lax.dot_general(rows, lagged_ref[...], contract, preferred_element_type=F32)
    lag_ref[...] = lag * scale - row_mean * means_ref[1, 0:1, :]


def vmem(count):
    return [pl.BlockSpec(memory_space=pltpu.VMEM)] * count


def solution(mesh):
    n = mesh.shape["tm"]
    n_rep = mesh.shape["rep"]

    def local(archive, swap_history, pair_index):
        steps, _, _, residues = archive.shape
        feats = pair_index.shape[1]
        width = feats // n
        per = n * steps
        raw = archive.reshape(steps * 3 * residues // LANES, LANES)
        dma = pltpu.SemaphoreType.DMA
        rows, cols, swaps = pl.pallas_call(
            functools.partial(exchange_kernel, n, n_rep),
            out_shape=[
                jax.ShapeDtypeStruct((n - 1, n, steps, width), BF16),
                jax.ShapeDtypeStruct((n, n, steps, width), BF16),
                jax.ShapeDtypeStruct((n, SUBLANES, per), F32),
            ],
            in_specs=[pl.BlockSpec(memory_space=pltpu.HBM)] * 3,
            out_specs=vmem(3),
            scratch_shapes=[pltpu.VMEM(raw.shape, F32), pltpu.VMEM(pair_index.shape, I32),
                            pltpu.VMEM(swap_history.shape[::-1], I32),
                            pltpu.VMEM((9 * steps, residues), BF16), pltpu.VMEM((n, steps, width), BF16),
                            pltpu.VMEM((SUBLANES, per), F32),
                            dma((n,)), dma((n,)), dma((n,)), dma((n,)),
                            dma((n, n)), dma((n, n)), dma((n, n)), dma((n, n)), dma((n, n)),
                            dma((n,)), dma((n,)), dma((3,))],
            compiler_params=pltpu.CompilerParams(
                collective_id=0, has_side_effects=True, vmem_limit_bytes=32 << 20),
        )(raw, pair_index, swap_history.T)
        tile = min(256, width)
        shape = jax.ShapeDtypeStruct((width, width), F32)
        return pl.pallas_call(
            functools.partial(covariance_kernel, (n - 1) * per),
            grid=(width // tile,),
            out_shape=[shape, shape],
            in_specs=[
                pl.BlockSpec((n - 1, per, tile), lambda r: (0, 0, r)),
                pl.BlockSpec((n, per, width), lambda r: (0, 0, 0)),
                pl.BlockSpec((n, SUBLANES, per), lambda r: (0, 0, 0)),
            ],
            out_specs=[pl.BlockSpec((tile, width), lambda r: (r, 0))] * 2,
            scratch_shapes=[pltpu.VMEM(((n - 1) * per, width), BF16), pltpu.VMEM((2, SUBLANES, width), F32)],
            compiler_params=pltpu.CompilerParams(vmem_limit_bytes=48 << 20),
        )(rows.reshape(n - 1, per, width), cols.reshape(n, per, width), swaps)

    return jax.shard_map(
        local,
        mesh=mesh,
        in_specs=(P(("grp", "tm"), ("feat", "rep"), None, None), P(("grp", "tm"), None), P()),
        out_specs=(P(("grp", "tm"), ("feat", "rep")), P(("grp", "tm"), ("feat", "rep"))),
        check_vma=False,
    )
```

```python
import functools

import jax
import jax.numpy as jnp
from jax import lax
from jax.experimental import pallas as pl
from jax.experimental.pallas import tpu as pltpu
from jax.sharding import PartitionSpec as P

LAG = 16
DIST_FLOOR = 0.3
LANES = 128
SUBLANES = 8
DEPTH = 256
BF16_MAX = float(jnp.finfo(jnp.bfloat16).max)
MESH = pl.DeviceIdType.MESH
BF16, F32, I32 = jnp.bfloat16, jnp.float32, jnp.int32


def pieces(value):
    high = jnp.clip(value, -BF16_MAX, BF16_MAX).astype(BF16)
    rest = value - high.astype(F32)
    middle = rest.astype(BF16)
    return high, middle, (rest - middle.astype(F32)).astype(BF16)


def feature_block(parts_ref, idx_ref, start, width, steps):
    count, residues = parts_ref.shape
    one, two = (idx_ref[side : side + 1, pl.ds(start, width)] for side in range(2))
    same = one == two
    one, two = jnp.where(same, -1, one), jnp.where(same, -1, two)
    shape = (DEPTH, width)
    residue = lax.broadcasted_iota(I32, shape, 0).astype(jnp.int16)
    plus, zero = jnp.ones(shape, BF16), jnp.zeros(shape, BF16)
    total = None
    for first in range(0, residues, DEPTH):
        at_one = residue == jnp.broadcast_to(one - first, shape).astype(jnp.int16)
        at_two = residue == jnp.broadcast_to(two - first, shape).astype(jnp.int16)
        chosen = jnp.where(at_one, plus, jnp.where(at_two, -plus, zero))
        part = jnp.dot(parts_ref[:, first : first + DEPTH], chosen, preferred_element_type=F32)
        total = part if total is None else total + part
    third = count // 3
    displace = total[:third] + total[third : 2 * third] + total[2 * third :]
    square = displace * displace
    square = square[:steps] + square[steps : 2 * steps] + square[2 * steps :]
    return (1.0 / jnp.maximum(jnp.sqrt(square), DIST_FLOOR)).astype(BF16)


def flat_swaps(swap):
    states, steps = swap.shape
    per = steps * states
    lane = lax.broadcasted_iota(I32, (steps, per), 1)
    spread = jnp.where(lane % steps == lax.broadcasted_iota(I32, (steps, per), 0), 1.0, 0.0)
    wide = jnp.dot(swap.astype(F32).astype(BF16), spread.astype(BF16), preferred_element_type=F32)
    lane = lax.broadcasted_iota(I32, (states, per), 1)
    mine = lane // steps == lax.broadcasted_iota(I32, (states, per), 0)
    row = jnp.sum(jnp.where(mine, wide, 0.0), axis=0, keepdims=True)
    return jnp.broadcast_to(row, (SUBLANES, per))


def exchange_kernel(n, n_rep, raw_hbm, idx_hbm, swap_hbm, rows_ref, cols_ref, swaps_ref,
                    raw, idx_ref, own_swap_ref, parts_ref, feat_ref, swap_ref,
                    s_row1, r_row1, s_col1, r_col1, s_row2, r_row2, s_col2, r_col2, s_sw, r_sw, own_sem):
    i0 = lax.axis_index("tm")
    g0 = lax.axis_index("feat") * n_rep + lax.axis_index("rep")
    is_lead = i0 < n - 1
    get_raw = pltpu.make_async_copy(raw_hbm, raw, own_sem.at[0])
    get_idx = pltpu.make_async_copy(idx_hbm, idx_ref, own_sem.at[1])
    get_raw.start()
    get_idx.start()
    get_swap = pltpu.make_async_copy(swap_hbm, own_swap_ref, own_sem.at[2])
    get_swap.start()

    def time_id(i):
        return {"tm": i}

    def group_id(j):
        return {"feat": j // n_rep, "rep": j % n_rep}

    def others(me, body):
        def step(d, carry):
            body((me + d) % n)
            return carry
        lax.fori_loop(1, n, step, 0)

    def remote(src, dst, send, recv, device):
        return pltpu.make_async_remote_copy(
            src_ref=src, dst_ref=dst, send_sem=send, recv_sem=recv, device_id=device, device_id_type=MESH)

    def row1(i):
        return remote(feat_ref.at[i], rows_ref.at[i0, g0], s_row1.at[i], r_row1.at[i0], time_id(i))

    def row1_in(i):
        return remote(feat_ref.at[i0], rows_ref.at[i, g0], s_row1.at[i], r_row1.at[i], time_id(i))

    def col1(j):
        return remote(feat_ref.at[j], cols_ref.at[i0, g0], s_col1.at[j], r_col1.at[g0], group_id(j))

    def col1_in(j):
        return remote(feat_ref.at[g0], cols_ref.at[i0, j], s_col1.at[j], r_col1.at[j], group_id(j))

    def row2(i, j):
        return remote(rows_ref.at[i, g0], rows_ref.at[i, g0], s_row2.at[i, j], r_row2.at[i, g0], group_id(j))

    def row2_in(i, j):
        return remote(rows_ref.at[i, j], rows_ref.at[i, j], s_row2.at[i, j], r_row2.at[i, j], group_id(j))

    def col2(i, j):
        return remote(cols_ref.at[i0, j], cols_ref.at[i0, j], s_col2.at[i, j], r_col2.at[i0, j], time_id(i))

    def col2_in(i, j):
        return remote(cols_ref.at[i, j], cols_ref.at[i, j], s_col2.at[i, j], r_col2.at[i, j], time_id(i))

    def swap(i):
        return remote(swap_ref, swaps_ref.at[i0], s_sw.at[i], r_sw.at[i0], time_id(i))

    def swap_in(i):
        return remote(swap_ref, swaps_ref.at[i], s_sw.at[i], r_sw.at[i], time_id(i))

    barrier = pltpu.get_barrier_semaphore()
    others(i0, lambda i: pl.semaphore_signal(barrier, inc=1, device_id=time_id(i), device_id_type=MESH))
    others(g0, lambda j: pl.semaphore_signal(barrier, inc=1, device_id=group_id(j), device_id_type=MESH))

    get_swap.wait()
    swap_ref[...] = flat_swaps(own_swap_ref[...])
    swaps_ref[i0] = swap_ref[...]
    count, residues = parts_ref.shape
    steps = feat_ref.shape[1]
    chunks = residues // LANES
    width = feat_ref.shape[2]
    get_raw.wait()
    for c in range(3):
        for h in range(chunks):
            rows = [raw[pl.ds((t * 3 + c) * chunks + h, SUBLANES, stride=3 * chunks), :]
                    for t in range(0, steps, SUBLANES)]
            for p, piece in enumerate(pieces(jnp.concatenate(rows, axis=0))):
                top = (p * 3 + c) * steps
                parts_ref[top : top + steps, h * LANES : (h + 1) * LANES] = piece
    get_idx.wait()
    pl.semaphore_wait(barrier, 2 * (n - 1))
    others(i0, lambda i: swap(i).start())

    def forward(k):
        @pl.when(k > 0)
        def _():
            j = (g0 - k + n) % n
            col1_in(j).wait_recv()
            others(i0, lambda to: col2(to, j).start())

        @pl.when((g0 + k) % n == i0)
        def _():
            def one(i):
                @pl.when(i < n - 1)
                def _():
                    row1_in(i).wait_recv()
                    others(g0, lambda to: row2(i, to).start())
            others(i0, one)

    def block(k, carry):
        b = (g0 + k) % n

        start = pl.multiple_of(b * width, LANES)
        feat_ref[b] = feature_block(parts_ref, idx_ref, start, width, steps)

        @pl.when(b != g0)
        def _():
            col1(b).start()

        @pl.when((b != i0) & is_lead)
        def _():
            row1(b).start()

        @pl.when(b == g0)
        def _():
            cols_ref[i0, g0] = feat_ref[b]
            others(i0, lambda to: col2(to, g0).start())

        @pl.when((b == i0) & is_lead)
        def _():
            rows_ref[i0, g0] = feat_ref[b]
            others(g0, lambda to: row2(i0, to).start())

        @pl.when(k > 0)
        def _():
            forward(k - 1)

        return carry

    lax.fori_loop(0, n, block, 0)
    forward(n - 1)

    def finish_swap(i):
        swap_in(i).wait_recv()
        swap(i).wait_send()

    others(i0, finish_swap)
    others(g0, lambda j: col1(j).wait_send())

    @pl.when(is_lead)
    def _():
        others(i0, lambda i: row1(i).wait_send())

    def end_rows(i, carry):
        def one(j):
            row2(i, j).wait_send()
            row2_in(i, j).wait_recv()
        others(g0, one)
        return carry

    lax.fori_loop(0, n - 1, end_rows, 0)

    def end_cols(j, carry):
        def one(i):
            col2(i, j).wait_send()
            col2_in(i, j).wait_recv()
        others(i0, one)
        return carry

    lax.fori_loop(0, n, end_cols, 0)


def covariance_kernel(frames, rows_ref, cols_ref, swaps_ref, inst_ref, lag_ref, lagged_ref, means_ref):
    blocks, per, _ = cols_ref.shape
    lead_rows = (blocks - 1) * per
    kept = lead_rows
    scale = 1.0 / frames

    @pl.when(pl.program_id(0) == 0)
    def _():
        here = lax.broadcasted_iota(I32, (per, per), 0) % LAG
        there = lax.broadcasted_iota(I32, (per, per), 1) % LAG
        same_step = here == there
        for i in range(blocks - 1):
            now = jnp.broadcast_to(swaps_ref[i, 0:1, :], (per, per)).T
            later = jnp.broadcast_to(swaps_ref[i + 1, 0:1, :], (per, per))
            pairs = jnp.where(same_step & (now == later), 1.0, 0.0).astype(BF16)
            lagged_ref[i * per : (i + 1) * per, :] = jnp.dot(
                pairs, cols_ref[i + 1], preferred_element_type=F32).astype(BF16)
        ones = jnp.ones((SUBLANES, kept), BF16)
        lead = cols_ref[: blocks - 1].reshape(kept, cols_ref.shape[2])
        means_ref[0] = jnp.dot(ones, lead, preferred_element_type=F32) * scale
        means_ref[1] = jnp.dot(ones, lagged_ref[...], preferred_element_type=F32) * scale

    rows = rows_ref[...].reshape(kept, rows_ref.shape[2])
    lead = cols_ref[: blocks - 1].reshape(kept, cols_ref.shape[2])
    contract = (((0,), (0,)), ((), ()))
    row_mean = lax.dot_general(rows, jnp.ones((kept, LANES), BF16), contract, preferred_element_type=F32)
    row_mean = row_mean[:, :1] * scale
    inst = lax.dot_general(rows, lead, contract, preferred_element_type=F32)
    inst_ref[...] = inst * scale - row_mean * means_ref[0, 0:1, :]
    lag = lax.dot_general(rows, lagged_ref[...], contract, preferred_element_type=F32)
    lag_ref[...] = lag * scale - row_mean * means_ref[1, 0:1, :]


def vmem(count):
    return [pl.BlockSpec(memory_space=pltpu.VMEM)] * count


def solution(mesh):
    n = mesh.shape["tm"]
    n_rep = mesh.shape["rep"]

    def local(archive, swap_history, pair_index):
        steps, _, _, residues = archive.shape
        feats = pair_index.shape[1]
        width = feats // n
        per = n * steps
        raw = archive.reshape(steps * 3 * residues // LANES, LANES)
        dma = pltpu.SemaphoreType.DMA
        rows, cols, swaps = pl.pallas_call(
            functools.partial(exchange_kernel, n, n_rep),
            out_shape=[
                jax.ShapeDtypeStruct((n - 1, n, steps, width), BF16),
                jax.ShapeDtypeStruct((n, n, steps, width), BF16),
                jax.ShapeDtypeStruct((n, SUBLANES, per), F32),
            ],
            in_specs=[pl.BlockSpec(memory_space=pltpu.HBM)] * 3,
            out_specs=vmem(3),
            scratch_shapes=[pltpu.VMEM(raw.shape, F32), pltpu.VMEM(pair_index.shape, I32),
                            pltpu.VMEM(swap_history.shape[::-1], I32),
                            pltpu.VMEM((9 * steps, residues), BF16), pltpu.VMEM((n, steps, width), BF16),
                            pltpu.VMEM((SUBLANES, per), F32),
                            dma((n,)), dma((n,)), dma((n,)), dma((n,)),
                            dma((n, n)), dma((n, n)), dma((n, n)), dma((n, n)),
                            dma((n,)), dma((n,)), dma((3,))],
            compiler_params=pltpu.CompilerParams(
                collective_id=0, has_side_effects=True, vmem_limit_bytes=60 << 20),
        )(raw, pair_index, swap_history.T)
        tile = min(256, width)
        shape = jax.ShapeDtypeStruct((width, width), F32)
        return pl.pallas_call(
            functools.partial(covariance_kernel, (n - 1) * per),
            grid=(width // tile,),
            out_shape=[shape, shape],
            in_specs=[
                pl.BlockSpec((n - 1, per, tile), lambda r: (0, 0, r)),
                pl.BlockSpec((n, per, width), lambda r: (0, 0, 0)),
                pl.BlockSpec((n, SUBLANES, per), lambda r: (0, 0, 0)),
            ],
            out_specs=[pl.BlockSpec((tile, width), lambda r: (r, 0))] * 2,
            scratch_shapes=[pltpu.VMEM(((n - 1) * per, width), BF16), pltpu.VMEM((2, SUBLANES, width), F32)],
            compiler_params=pltpu.CompilerParams(vmem_limit_bytes=60 << 20),
        )(rows.reshape(n - 1, per, width), cols.reshape(n, per, width), swaps)

    return jax.shard_map(
        local,
        mesh=mesh,
        in_specs=(P(("grp", "tm"), ("feat", "rep"), None, None), P(("grp", "tm"), None), P()),
        out_specs=(P(("grp", "tm"), ("feat", "rep")), P(("grp", "tm"), ("feat", "rep"))),
        check_vma=False,
    )
```

```python
import functools

import jax
import jax.numpy as jnp
from jax import lax
from jax.experimental import pallas as pl
from jax.experimental.pallas import tpu as pltpu
from jax.sharding import PartitionSpec as P

LAG = 16
DIST_FLOOR = 0.3
LANES = 128
SUBLANES = 8
DEPTH = 256
BF16_MAX = float(jnp.finfo(jnp.bfloat16).max)
MESH = pl.DeviceIdType.MESH
BF16, F32, I32 = jnp.bfloat16, jnp.float32, jnp.int32


def pieces(value):
    high = jnp.clip(value, -BF16_MAX, BF16_MAX).astype(BF16)
    rest = value - high.astype(F32)
    middle = rest.astype(BF16)
    return high, middle, (rest - middle.astype(F32)).astype(BF16)


def feature_block(parts_ref, idx_ref, start, width, steps):
    count, residues = parts_ref.shape
    one, two = (idx_ref[side : side + 1, pl.ds(start, width)] for side in range(2))
    same = one == two
    one, two = jnp.where(same, -1, one), jnp.where(same, -1, two)
    shape = (DEPTH, width)
    residue = lax.broadcasted_iota(I32, shape, 0).astype(jnp.int16)
    plus, zero = jnp.ones(shape, BF16), jnp.zeros(shape, BF16)
    total = None
    for first in range(0, residues, DEPTH):
        at_one = residue == jnp.broadcast_to(one - first, shape).astype(jnp.int16)
        at_two = residue == jnp.broadcast_to(two - first, shape).astype(jnp.int16)
        chosen = jnp.where(at_one, plus, jnp.where(at_two, -plus, zero))
        part = jnp.dot(parts_ref[:, first : first + DEPTH], chosen, preferred_element_type=F32)
        total = part if total is None else total + part
    third = count // 3
    displace = total[:third] + total[third : 2 * third] + total[2 * third :]
    square = displace * displace
    square = square[:steps] + square[steps : 2 * steps] + square[2 * steps :]
    return (1.0 / jnp.maximum(jnp.sqrt(square), DIST_FLOOR)).astype(BF16)


def flat_swaps(swap):
    states, steps = swap.shape
    per = steps * states
    lane = lax.broadcasted_iota(I32, (steps, per), 1)
    spread = jnp.where(lane % steps == lax.broadcasted_iota(I32, (steps, per), 0), 1.0, 0.0)
    wide = jnp.dot(swap.astype(F32).astype(BF16), spread.astype(BF16), preferred_element_type=F32)
    lane = lax.broadcasted_iota(I32, (states, per), 1)
    mine = lane // steps == lax.broadcasted_iota(I32, (states, per), 0)
    row = jnp.sum(jnp.where(mine, wide, 0.0), axis=0, keepdims=True)
    return jnp.broadcast_to(row, (SUBLANES, per))


def exchange_kernel(n, n_rep, raw_hbm, idx_hbm, swap_hbm, rows_ref, cols_ref, swaps_ref,
                    raw, idx_ref, own_swap_ref, parts_ref, feat_ref, swap_ref,
                    s_row1, r_row1, s_col1, r_col1, s_row2, r_row2, s_col2, r_col2, s_sw, r_sw, own_sem):
    i0 = lax.axis_index("tm")
    g0 = lax.axis_index("feat") * n_rep + lax.axis_index("rep")
    is_lead = i0 < n - 1
    get_raw = pltpu.make_async_copy(raw_hbm, raw, own_sem.at[0])
    get_idx = pltpu.make_async_copy(idx_hbm, idx_ref, own_sem.at[1])
    get_raw.start()
    get_idx.start()
    get_swap = pltpu.make_async_copy(swap_hbm, own_swap_ref, own_sem.at[2])
    get_swap.start()

    def time_id(i):
        return {"tm": i}

    def group_id(j):
        return {"feat": j // n_rep, "rep": j % n_rep}

    def others(me, body):
        def step(d, carry):
            body((me + d) % n)
            return carry
        lax.fori_loop(1, n, step, 0)

    def remote(src, dst, send, recv, device):
        return pltpu.make_async_remote_copy(
            src_ref=src, dst_ref=dst, send_sem=send, recv_sem=recv, device_id=device, device_id_type=MESH)

    def row1(i):
        return remote(feat_ref.at[i], rows_ref.at[i0, g0], s_row1.at[i], r_row1.at[i0], time_id(i))

    def row1_in(i):
        return remote(feat_ref.at[i0], rows_ref.at[i, g0], s_row1.at[i], r_row1.at[i], time_id(i))

    def col1(j):
        return remote(feat_ref.at[j], cols_ref.at[i0, g0], s_col1.at[j], r_col1.at[g0], group_id(j))

    def col1_in(j):
        return remote(feat_ref.at[g0], cols_ref.at[i0, j], s_col1.at[j], r_col1.at[j], group_id(j))

    def row2(i, j):
        return remote(rows_ref.at[i, g0], rows_ref.at[i, g0], s_row2.at[i, j], r_row2.at[i, g0], group_id(j))

    def row2_in(i, j):
        return remote(rows_ref.at[i, j], rows_ref.at[i, j], s_row2.at[i, j], r_row2.at[i, j], group_id(j))

    def col2(i, j):
        return remote(cols_ref.at[i0, j], cols_ref.at[i0, j], s_col2.at[i, j], r_col2.at[i0, j], time_id(i))

    def col2_in(i, j):
        return remote(cols_ref.at[i, j], cols_ref.at[i, j], s_col2.at[i, j], r_col2.at[i, j], time_id(i))

    def swap(i):
        return remote(swap_ref, swaps_ref.at[i0], s_sw.at[i], r_sw.at[i0], time_id(i))

    def swap_in(i):
        return remote(swap_ref, swaps_ref.at[i], s_sw.at[i], r_sw.at[i], time_id(i))

    barrier = pltpu.get_barrier_semaphore()
    others(i0, lambda i: pl.semaphore_signal(barrier, inc=1, device_id=time_id(i), device_id_type=MESH))
    others(g0, lambda j: pl.semaphore_signal(barrier, inc=1, device_id=group_id(j), device_id_type=MESH))

    get_swap.wait()
    swap_ref[...] = flat_swaps(own_swap_ref[...])
    swaps_ref[i0] = swap_ref[...]
    count, residues = parts_ref.shape
    steps = feat_ref.shape[1]
    chunks = residues // LANES
    width = feat_ref.shape[2]
    get_raw.wait()
    for c in range(3):
        for h in range(chunks):
            rows = [raw[pl.ds((t * 3 + c) * chunks + h, SUBLANES, stride=3 * chunks), :]
                    for t in range(0, steps, SUBLANES)]
            for p, piece in enumerate(pieces(jnp.concatenate(rows, axis=0))):
                top = (p * 3 + c) * steps
                parts_ref[top : top + steps, h * LANES : (h + 1) * LANES] = piece
    get_idx.wait()
    pl.semaphore_wait(barrier, 2 * (n - 1))
    others(i0, lambda i: swap(i).start())

    def forward(k):
        j = (g0 - i0 - k + 2 * n) % n
        i = (i0 - g0 - k + 2 * n) % n

        @pl.when(j != g0)
        def _():
            col1_in(j).wait_recv()
            others(i0, lambda to: col2(to, j).start())

        @pl.when((i != i0) & (i < n - 1))
        def _():
            row1_in(i).wait_recv()
            others(g0, lambda to: row2(i, to).start())

    def block(k, carry):
        b = (i0 + g0 + k) % n

        start = pl.multiple_of(b * width, LANES)
        feat_ref[b] = feature_block(parts_ref, idx_ref, start, width, steps)

        @pl.when(b != g0)
        def _():
            col1(b).start()

        @pl.when((b != i0) & is_lead)
        def _():
            row1(b).start()

        @pl.when(b == g0)
        def _():
            cols_ref[i0, g0] = feat_ref[b]
            others(i0, lambda to: col2(to, g0).start())

        @pl.when((b == i0) & is_lead)
        def _():
            rows_ref[i0, g0] = feat_ref[b]
            others(g0, lambda to: row2(i0, to).start())

        @pl.when(k > 0)
        def _():
            forward(k - 1)

        return carry

    lax.fori_loop(0, n, block, 0)
    forward(n - 1)

    def finish_swap(i):
        swap_in(i).wait_recv()
        swap(i).wait_send()

    others(i0, finish_swap)
    others(g0, lambda j: col1(j).wait_send())

    @pl.when(is_lead)
    def _():
        others(i0, lambda i: row1(i).wait_send())

    def end_rows(i, carry):
        def one(j):
            row2(i, j).wait_send()
            row2_in(i, j).wait_recv()
        others(g0, one)
        return carry

    lax.fori_loop(0, n - 1, end_rows, 0)

    def end_cols(j, carry):
        def one(i):
            col2(i, j).wait_send()
            col2_in(i, j).wait_recv()
        others(i0, one)
        return carry

    lax.fori_loop(0, n, end_cols, 0)


def covariance_kernel(frames, rows_ref, cols_ref, swaps_ref, inst_ref, lag_ref, lagged_ref, means_ref):
    blocks, per, _ = cols_ref.shape
    lead_rows = (blocks - 1) * per
    kept = lead_rows
    scale = 1.0 / frames

    @pl.when(pl.program_id(0) == 0)
    def _():
        here = lax.broadcasted_iota(I32, (per, per), 0) % LAG
        there = lax.broadcasted_iota(I32, (per, per), 1) % LAG
        same_step = here == there
        for i in range(blocks - 1):
            now = jnp.broadcast_to(swaps_ref[i, 0:1, :], (per, per)).T
            later = jnp.broadcast_to(swaps_ref[i + 1, 0:1, :], (per, per))
            pairs = jnp.where(same_step & (now == later), 1.0, 0.0).astype(BF16)
            lagged_ref[i * per : (i + 1) * per, :] = jnp.dot(
                pairs, cols_ref[i + 1], preferred_element_type=F32).astype(BF16)
        ones = jnp.ones((SUBLANES, kept), BF16)
        lead = cols_ref[: blocks - 1].reshape(kept, cols_ref.shape[2])
        means_ref[0] = jnp.dot(ones, lead, preferred_element_type=F32) * scale
        means_ref[1] = jnp.dot(ones, lagged_ref[...], preferred_element_type=F32) * scale

    rows = rows_ref[...].reshape(kept, rows_ref.shape[2])
    lead = cols_ref[: blocks - 1].reshape(kept, cols_ref.shape[2])
    contract = (((0,), (0,)), ((), ()))
    row_mean = lax.dot_general(rows, jnp.ones((kept, LANES), BF16), contract, preferred_element_type=F32)
    row_mean = row_mean[:, :1] * scale
    inst = lax.dot_general(rows, lead, contract, preferred_element_type=F32)
    inst_ref[...] = inst * scale - row_mean * means_ref[0, 0:1, :]
    lag = lax.dot_general(rows, lagged_ref[...], contract, preferred_element_type=F32)
    lag_ref[...] = lag * scale - row_mean * means_ref[1, 0:1, :]


def vmem(count):
    return [pl.BlockSpec(memory_space=pltpu.VMEM)] * count


def solution(mesh):
    n = mesh.shape["tm"]
    n_rep = mesh.shape["rep"]

    def local(archive, swap_history, pair_index):
        steps, _, _, residues = archive.shape
        feats = pair_index.shape[1]
        width = feats // n
        per = n * steps
        raw = archive.reshape(steps * 3 * residues // LANES, LANES)
        dma = pltpu.SemaphoreType.DMA
        rows, cols, swaps = pl.pallas_call(
            functools.partial(exchange_kernel, n, n_rep),
            out_shape=[
                jax.ShapeDtypeStruct((n - 1, n, steps, width), BF16),
                jax.ShapeDtypeStruct((n, n, steps, width), BF16),
                jax.ShapeDtypeStruct((n, SUBLANES, per), F32),
            ],
            in_specs=[pl.BlockSpec(memory_space=pltpu.HBM)] * 3,
            out_specs=vmem(3),
            scratch_shapes=[pltpu.VMEM(raw.shape, F32), pltpu.VMEM(pair_index.shape, I32),
                            pltpu.VMEM(swap_history.shape[::-1], I32),
                            pltpu.VMEM((9 * steps, residues), BF16), pltpu.VMEM((n, steps, width), BF16),
                            pltpu.VMEM((SUBLANES, per), F32),
                            dma((n,)), dma((n,)), dma((n,)), dma((n,)),
                            dma((n, n)), dma((n, n)), dma((n, n)), dma((n, n)),
                            dma((n,)), dma((n,)), dma((3,))],
            compiler_params=pltpu.CompilerParams(
                collective_id=0, has_side_effects=True, vmem_limit_bytes=60 << 20),
        )(raw, pair_index, swap_history.T)
        tile = min(LANES, width)
        shape = jax.ShapeDtypeStruct((width, width), F32)
        return pl.pallas_call(
            functools.partial(covariance_kernel, (n - 1) * per),
            grid=(width // tile,),
            out_shape=[shape, shape],
            in_specs=[
                pl.BlockSpec((n - 1, per, tile), lambda r: (0, 0, r)),
                pl.BlockSpec((n, per, width), lambda r: (0, 0, 0)),
                pl.BlockSpec((n, SUBLANES, per), lambda r: (0, 0, 0)),
            ],
            out_specs=[pl.BlockSpec((tile, width), lambda r: (r, 0))] * 2,
            scratch_shapes=[pltpu.VMEM(((n - 1) * per, width), BF16), pltpu.VMEM((2, SUBLANES, width), F32)],
            compiler_params=pltpu.CompilerParams(vmem_limit_bytes=60 << 20),
        )(rows.reshape(n - 1, per, width), cols.reshape(n, per, width), swaps)

    return jax.shard_map(
        local,
        mesh=mesh,
        in_specs=(P(("grp", "tm"), ("feat", "rep"), None, None), P(("grp", "tm"), None), P()),
        out_specs=(P(("grp", "tm"), ("feat", "rep")), P(("grp", "tm"), ("feat", "rep"))),
        check_vma=False,
    )
```

```python
import functools

import jax
import jax.numpy as jnp
from jax import lax
from jax.experimental import pallas as pl
from jax.experimental.pallas import tpu as pltpu
from jax.sharding import PartitionSpec as P

LAG = 16
DIST_FLOOR = 0.3
LANES = 128
SUBLANES = 8
DEPTH = 256
BF16_MAX = float(jnp.finfo(jnp.bfloat16).max)
MESH = pl.DeviceIdType.MESH
BF16, F32, I32 = jnp.bfloat16, jnp.float32, jnp.int32


def pieces(value):
    high = jnp.clip(value, -BF16_MAX, BF16_MAX).astype(BF16)
    rest = value - high.astype(F32)
    middle = rest.astype(BF16)
    return high, middle, (rest - middle.astype(F32)).astype(BF16)


def feature_block(parts_ref, idx_ref, start, width, steps):
    count, residues = parts_ref.shape
    one, two = (idx_ref[side : side + 1, pl.ds(start, width)] for side in range(2))
    same = one == two
    one, two = jnp.where(same, -1, one), jnp.where(same, -1, two)
    shape = (DEPTH, width)
    residue = lax.broadcasted_iota(I32, shape, 0).astype(jnp.int16)
    plus, zero = jnp.ones(shape, BF16), jnp.zeros(shape, BF16)
    total = None
    for first in range(0, residues, DEPTH):
        at_one = residue == jnp.broadcast_to(one - first, shape).astype(jnp.int16)
        at_two = residue == jnp.broadcast_to(two - first, shape).astype(jnp.int16)
        chosen = jnp.where(at_one, plus, jnp.where(at_two, -plus, zero))
        part = jnp.dot(parts_ref[:, first : first + DEPTH], chosen, preferred_element_type=F32)
        total = part if total is None else total + part
    third = count // 3
    displace = total[:third] + total[third : 2 * third] + total[2 * third :]
    square = displace * displace
    square = square[:steps] + square[steps : 2 * steps] + square[2 * steps :]
    return (1.0 / jnp.maximum(jnp.sqrt(square), DIST_FLOOR)).astype(BF16)


def flat_swaps(swap):
    states, steps = swap.shape
    per = steps * states
    lane = lax.broadcasted_iota(I32, (steps, per), 1)
    spread = jnp.where(lane % steps == lax.broadcasted_iota(I32, (steps, per), 0), 1.0, 0.0)
    wide = jnp.dot(swap.astype(F32).astype(BF16), spread.astype(BF16), preferred_element_type=F32)
    lane = lax.broadcasted_iota(I32, (states, per), 1)
    mine = lane // steps == lax.broadcasted_iota(I32, (states, per), 0)
    row = jnp.sum(jnp.where(mine, wide, 0.0), axis=0, keepdims=True)
    return jnp.broadcast_to(row, (SUBLANES, per))


def exchange_kernel(n, n_rep, raw_ref, idx_hbm, swap_in_ref, rows_ref, cols_ref, swaps_ref,
                    raw, idx_ref, parts_ref, feat_ref, swap_ref,
                    s_row1, r_row1, s_col1, r_col1, s_row2, r_row2, s_col2, r_col2, s_sw, r_sw, own_sem):
    i0 = lax.axis_index("tm")
    g0 = lax.axis_index("feat") * n_rep + lax.axis_index("rep")
    is_lead = i0 < n - 1
    get_raw = pltpu.make_async_copy(raw_ref, raw, own_sem.at[0])
    get_idx = pltpu.make_async_copy(idx_hbm, idx_ref, own_sem.at[1])
    get_raw.start()
    get_idx.start()

    def time_id(i):
        return {"tm": i}

    def group_id(j):
        return {"feat": j // n_rep, "rep": j % n_rep}

    def others(me, body):
        def step(d, carry):
            body((me + d) % n)
            return carry
        lax.fori_loop(1, n, step, 0)

    def remote(src, dst, send, recv, device):
        return pltpu.make_async_remote_copy(
            src_ref=src, dst_ref=dst, send_sem=send, recv_sem=recv, device_id=device, device_id_type=MESH)

    def row1(i):
        return remote(feat_ref.at[i], rows_ref.at[i0, g0], s_row1.at[i], r_row1.at[i0], time_id(i))

    def row1_in(i):
        return remote(feat_ref.at[i0], rows_ref.at[i, g0], s_row1.at[i], r_row1.at[i], time_id(i))

    def col1(j):
        return remote(feat_ref.at[j], cols_ref.at[i0, g0], s_col1.at[j], r_col1.at[g0], group_id(j))

    def col1_in(j):
        return remote(feat_ref.at[g0], cols_ref.at[i0, j], s_col1.at[j], r_col1.at[j], group_id(j))

    def row2(i, j):
        return remote(rows_ref.at[i, g0], rows_ref.at[i, g0], s_row2.at[i, j], r_row2.at[i, g0], group_id(j))

    def row2_in(i, j):
        return remote(rows_ref.at[i, j], rows_ref.at[i, j], s_row2.at[i, j], r_row2.at[i, j], group_id(j))

    def col2(i, j):
        return remote(cols_ref.at[i0, j], cols_ref.at[i0, j], s_col2.at[i, j], r_col2.at[i0, j], time_id(i))

    def col2_in(i, j):
        return remote(cols_ref.at[i, j], cols_ref.at[i, j], s_col2.at[i, j], r_col2.at[i, j], time_id(i))

    def swap(i):
        return remote(swap_ref, swaps_ref.at[i0], s_sw.at[i], r_sw.at[i0], time_id(i))

    def swap_in(i):
        return remote(swap_ref, swaps_ref.at[i], s_sw.at[i], r_sw.at[i], time_id(i))

    barrier = pltpu.get_barrier_semaphore()
    others(i0, lambda i: pl.semaphore_signal(barrier, inc=1, device_id=time_id(i), device_id_type=MESH))
    others(g0, lambda j: pl.semaphore_signal(barrier, inc=1, device_id=group_id(j), device_id_type=MESH))

    swap_ref[...] = flat_swaps(swap_in_ref[...])
    swaps_ref[i0] = swap_ref[...]
    count, residues = parts_ref.shape
    steps = feat_ref.shape[1]
    chunks = residues // LANES
    width = feat_ref.shape[2]
    get_raw.wait()
    for c in range(3):
        for h in range(chunks):
            rows = [raw[pl.ds((t * 3 + c) * chunks + h, SUBLANES, stride=3 * chunks), :]
                    for t in range(0, steps, SUBLANES)]
            for p, piece in enumerate(pieces(jnp.concatenate(rows, axis=0))):
                top = (p * 3 + c) * steps
                parts_ref[top : top + steps, h * LANES : (h + 1) * LANES] = piece
    get_idx.wait()
    pl.semaphore_wait(barrier, 2 * (n - 1))
    others(i0, lambda i: swap(i).start())

    def forward(k):
        j = (g0 - i0 - k + 2 * n) % n
        i = (i0 - g0 - k + 2 * n) % n

        @pl.when(j != g0)
        def _():
            col1_in(j).wait_recv()
            others(i0, lambda to: col2(to, j).start())

        @pl.when((i != i0) & (i < n - 1))
        def _():
            row1_in(i).wait_recv()
            others(g0, lambda to: row2(i, to).start())

    def block(k, carry):
        b = (i0 + g0 + k) % n

        start = pl.multiple_of(b * width, LANES)
        feat_ref[b] = feature_block(parts_ref, idx_ref, start, width, steps)

        @pl.when(b != g0)
        def _():
            col1(b).start()

        @pl.when((b != i0) & is_lead)
        def _():
            row1(b).start()

        @pl.when(b == g0)
        def _():
            cols_ref[i0, g0] = feat_ref[b]
            others(i0, lambda to: col2(to, g0).start())

        @pl.when((b == i0) & is_lead)
        def _():
            rows_ref[i0, g0] = feat_ref[b]
            others(g0, lambda to: row2(i0, to).start())

        @pl.when(k > 0)
        def _():
            forward(k - 1)

        return carry

    lax.fori_loop(0, n, block, 0)
    forward(n - 1)

    def finish_swap(i):
        swap_in(i).wait_recv()
        swap(i).wait_send()

    others(i0, finish_swap)
    others(g0, lambda j: col1(j).wait_send())

    @pl.when(is_lead)
    def _():
        others(i0, lambda i: row1(i).wait_send())

    def end_rows(i, carry):
        def one(j):
            row2(i, j).wait_send()
            row2_in(i, j).wait_recv()
        others(g0, one)
        return carry

    lax.fori_loop(0, n - 1, end_rows, 0)

    def end_cols(j, carry):
        def one(i):
            col2(i, j).wait_send()
            col2_in(i, j).wait_recv()
        others(i0, one)
        return carry

    lax.fori_loop(0, n, end_cols, 0)


def covariance_kernel(frames, rows_ref, cols_ref, swaps_ref, inst_ref, lag_ref, lagged_ref, means_ref):
    blocks, per, _ = cols_ref.shape
    lead_rows = (blocks - 1) * per
    kept = lead_rows
    scale = 1.0 / frames

    @pl.when(pl.program_id(0) == 0)
    def _():
        here = lax.broadcasted_iota(I32, (per, per), 0) % LAG
        there = lax.broadcasted_iota(I32, (per, per), 1) % LAG
        same_step = here == there
        for i in range(blocks - 1):
            now = jnp.broadcast_to(swaps_ref[i, 0:1, :], (per, per)).T
            later = jnp.broadcast_to(swaps_ref[i + 1, 0:1, :], (per, per))
            pairs = jnp.where(same_step & (now == later), 1.0, 0.0).astype(BF16)
            lagged_ref[i * per : (i + 1) * per, :] = jnp.dot(
                pairs, cols_ref[i + 1], preferred_element_type=F32).astype(BF16)
        ones = jnp.ones((SUBLANES, kept), BF16)
        lead = cols_ref[: blocks - 1].reshape(kept, cols_ref.shape[2])
        means_ref[0] = jnp.dot(ones, lead, preferred_element_type=F32) * scale
        means_ref[1] = jnp.dot(ones, lagged_ref[...], preferred_element_type=F32) * scale

    rows = rows_ref[...].reshape(kept, rows_ref.shape[2])
    lead = cols_ref[: blocks - 1].reshape(kept, cols_ref.shape[2])
    contract = (((0,), (0,)), ((), ()))
    row_mean = lax.dot_general(rows, jnp.ones((kept, LANES), BF16), contract, preferred_element_type=F32)
    row_mean = row_mean[:, :1] * scale
    inst = lax.dot_general(rows, lead, contract, preferred_element_type=F32)
    inst_ref[...] = inst * scale - row_mean * means_ref[0, 0:1, :]
    lag = lax.dot_general(rows, lagged_ref[...], contract, preferred_element_type=F32)
    lag_ref[...] = lag * scale - row_mean * means_ref[1, 0:1, :]


def vmem(count):
    return [pl.BlockSpec(memory_space=pltpu.VMEM)] * count


def solution(mesh):
    n = mesh.shape["tm"]
    n_rep = mesh.shape["rep"]

    def local(archive, swap_history, pair_index):
        steps, _, _, residues = archive.shape
        feats = pair_index.shape[1]
        width = feats // n
        per = n * steps
        raw = archive.reshape(steps * 3 * residues // LANES, LANES)
        dma = pltpu.SemaphoreType.DMA
        rows, cols, swaps = pl.pallas_call(
            functools.partial(exchange_kernel, n, n_rep),
            out_shape=[
                jax.ShapeDtypeStruct((n - 1, n, steps, width), BF16),
                jax.ShapeDtypeStruct((n, n, steps, width), BF16),
                jax.ShapeDtypeStruct((n, SUBLANES, per), F32),
            ],
            in_specs=[pl.BlockSpec(memory_space=pl.ANY)] * 2 + vmem(1),
            out_specs=vmem(3),
            scratch_shapes=[pltpu.VMEM(raw.shape, F32), pltpu.VMEM(pair_index.shape, I32),
                            pltpu.VMEM((9 * steps, residues), BF16), pltpu.VMEM((n, steps, width), BF16),
                            pltpu.VMEM((SUBLANES, per), F32),
                            dma((n,)), dma((n,)), dma((n,)), dma((n,)),
                            dma((n, n)), dma((n, n)), dma((n, n)), dma((n, n)),
                            dma((n,)), dma((n,)), dma((2,))],
            compiler_params=pltpu.CompilerParams(
                collective_id=0, has_side_effects=True, vmem_limit_bytes=32 << 20),
        )(raw, pair_index, swap_history.T)
        tile = min(512, width)
        shape = jax.ShapeDtypeStruct((width, width), F32)
        return pl.pallas_call(
            functools.partial(covariance_kernel, (n - 1) * per),
            grid=(width // tile,),
            out_shape=[shape, shape],
            in_specs=[
                pl.BlockSpec((n - 1, per, tile), lambda r: (0, 0, r)),
                pl.BlockSpec((n, per, width), lambda r: (0, 0, 0)),
                pl.BlockSpec((n, SUBLANES, per), lambda r: (0, 0, 0)),
            ],
            out_specs=[pl.BlockSpec((tile, width), lambda r: (r, 0))] * 2,
            scratch_shapes=[pltpu.VMEM(((n - 1) * per, width), BF16), pltpu.VMEM((2, SUBLANES, width), F32)],
            compiler_params=pltpu.CompilerParams(vmem_limit_bytes=48 << 20),
        )(rows.reshape(n - 1, per, width), cols.reshape(n, per, width), swaps)

    return jax.shard_map(
        local,
        mesh=mesh,
        in_specs=(P(("grp", "tm"), ("feat", "rep"), None, None), P(("grp", "tm"), None), P()),
        out_specs=(P(("grp", "tm"), ("feat", "rep")), P(("grp", "tm"), ("feat", "rep"))),
        check_vma=False,
    )
```
